32 devices in a mesh: dom: 8 (over z, y), src: 4 (over x, core).
Axes of the slice: x: 2, y: 2, z: 4, core: 2. Of those that a mesh axis runs over, the one named last changes fastest.
Arguments:
- features: bfloat16 [32768, 256], P(('dom', 'src')), may hold values from -6 to 6
- cotangent: bfloat16 [32768, 256], P(('dom', 'src')), may hold values from -6 to 6
- w_self: bfloat16 [256, 256], replicated, may hold values from -0.375 to 0.375
- w_neigh: bfloat16 [256, 256], replicated, may hold values from -0.375 to 0.375
- bias: bfloat16 [256], replicated, may hold values from -3 to 3
- send_rows: int32 [8, 4, 8, 8], P('dom', 'src'), may hold values from -1 to 1023, as said below
- edge_src: int32 [8, 4, 8192], P('dom', 'src'), may hold values from 0 to 1087, as said below
- edge_dst: int32 [8, 4, 8192], P('dom', 'src'), may hold values from 0 to 4095
- tile_count: int32 [8, 4], P('dom', 'src'), may hold values from 16 to 64, as said below
Outputs:
- activations: bfloat16 [32768, 256], P(('dom', 'src'))
- feature_grad: float32 [32768, 256], P(('dom', 'src'))
The draws below stay inside these ranges and needn't reach their ends.
Inputs may be any that keep to these rules, and one draw needn't show every extreme that they name: `send_rows`: slots of a list are filled from the first one; some list of every owner is full; an account's own part sends it nothing. `edge_src`: every edge refers to a local row or to a filled slot. Edge slots after the first tile_count * 128 are ignored.
All inputs are finite; a program needn't handle non-finite values.
Results may differ from the reference program's by a relative error of at most 0.009.
Values may be sent and summed in bfloat16 or wider, within the bound.
A program may use at most 64 MiB of HBM per device.

```python
import jax
import jax.numpy as jnp
from jax import lax

F = 256
H = 256
TILE = 128
NODE_DEV = 1024
CAP = 8
TILES_DEV = 64
E_DEV = 8192
PART_ROWS = 4096
HALO = 64
NODES = 32768
N_DOM = 8
N_SRC = 4


def peer_counts(key):
    counts = jax.random.randint(jax.random.fold_in(key, 101), (N_DOM, N_SRC, N_DOM), 1, CAP + 1)
    owner = jnp.arange(N_DOM)[:, None, None]
    reader = jnp.arange(N_DOM)[None, None, :]
    counts = jnp.where(owner == reader, 0, counts)
    counts = jnp.where(reader == (owner + 1) % N_DOM, CAP, counts)
    return counts


def draw_send_rows(key, part):
    counts = peer_counts(key)
    chosen = jax.random.randint(jax.random.fold_in(key, 211), (N_DOM, N_SRC, N_DOM, CAP), 0, NODE_DEV)
    slot_index = jnp.arange(CAP)[None, None, None, :]
    return jnp.where(slot_index < counts[:, :, :, None], chosen, -1).astype(jnp.int32)


def draw_edge_src(key, part):
    counts = peer_counts(key)
    shape = (N_DOM, N_SRC, E_DEV)
    reader = jnp.arange(N_DOM)[:, None, None] + jnp.zeros(shape, jnp.int32)
    column = jnp.arange(N_SRC)[None, :, None] + jnp.zeros(shape, jnp.int32)
    local_pick = jax.random.randint(jax.random.fold_in(key, 307), shape, 0, NODE_DEV)
    offset = jax.random.randint(jax.random.fold_in(key, 311), shape, 0, N_DOM - 1)
    owner = (reader + 1 + offset) % N_DOM
    limit = counts[owner, column, reader]
    slot_pick = jax.random.randint(jax.random.fold_in(key, 313), shape, 0, limit)
    remote_pick = NODE_DEV + owner * CAP + slot_pick
    coin = jax.random.randint(jax.random.fold_in(key, 317), shape, 0, 2)
    result = jnp.where(coin == 0, local_pick, remote_pick)
    result = result.at[0, :, 0].set(NODE_DEV + (N_DOM - 1) * CAP + CAP - 1)
    return result.astype(jnp.int32)


def draw_tile_count(key, part):
    lowest = max(1, TILES_DEV // 4)
    counts = jax.random.randint(jax.random.fold_in(key, 401), (N_DOM * N_SRC,), lowest, TILES_DEV + 1)
    busiest = jax.random.randint(jax.random.fold_in(key, 409), (), 0, N_DOM * N_SRC)
    counts = counts.at[busiest].set(TILES_DEV)
    return counts.reshape(N_DOM, N_SRC).astype(jnp.int32)


def touch_ends(drawn, key, low, top_value):
    longest = drawn.shape.index(max(drawn.shape))
    spots = []
    for shift in (0, 1):
        where = [jax.random.randint(jax.random.fold_in(key, axis), (), 0, length) for axis, length in enumerate(drawn.shape)]
        where[longest] = (where[longest] + shift) % drawn.shape[longest]
        spots.append(tuple(where))
    return drawn.at[spots[0]].set(low).at[spots[1]].set(top_value)


def shard_levels(rng, extent, split, least, largest):
    factor_of = 1.0
    for axis_at, parts in split:
        draws = jax.random.uniform(jax.random.fold_in(jax.random.fold_in(rng, 6), axis_at), (parts,), jnp.float32, least / len(split), largest / len(split))
        factor_of = factor_of * jnp.repeat(jnp.exp(draws), extent[axis_at] // parts).reshape((-1,) + (1,) * (len(extent) - 1 - axis_at))
    return factor_of


def normal_values(stream_key, extent, width, most, shards=(), dtype=jnp.bfloat16):
    entries = jax.random.normal(stream_key, extent, jnp.float32) * width
    if len(shards) > 0:
        entries = shard_levels(stream_key, extent, shards, -0.22, 0.18) * entries
    return jnp.clip(entries, min=-most, max=most).astype(dtype)


def setup_inputs(seed: int = 0) -> dict:
    seeds = jax.random.split(jax.random.key(seed), 10)
    return {
        "features": normal_values(seeds[0], (NODES, F), 1.0, 6.0, ((0, 32),)),
        "cotangent": normal_values(seeds[1], (NODES, H), 1.0, 6.0, ((0, 32),)),
        "w_self": normal_values(seeds[2], (F, H), F ** -0.5, 0.375),
        "w_neigh": normal_values(seeds[3], (F, H), F ** -0.5, 0.375),
        "bias": normal_values(seeds[4], (H,), 0.5, 3.0),
        "send_rows": draw_send_rows(jax.random.fold_in(seeds[9], 71), 0),
        "edge_src": draw_edge_src(jax.random.fold_in(seeds[9], 71), 0),
        "edge_dst": touch_ends(jax.random.randint(seeds[7], (N_DOM, N_SRC, E_DEV), 0, PART_ROWS), jax.random.fold_in(seeds[7], 1), 0, PART_ROWS - 1).astype(jnp.int32),
        "tile_count": draw_tile_count(jax.random.fold_in(seeds[9], 71), 0),
    }


def reference(features, cotangent, w_self, w_neigh, bias, send_rows, edge_src, edge_dst, tile_count):
    blocks = features.reshape(N_DOM, N_SRC, NODE_DEV, F)
    upstreams = cotangent.reshape(N_DOM, N_SRC, NODE_DEV, H)
    peer_index = jnp.arange(N_DOM)
    edge_tile = jnp.arange(E_DEV) // TILE

    def column_data(owner, column):
        senders = send_rows[:, column, owner, :]
        filled = senders >= 0
        active = edge_tile < tile_count[owner, column]
        return senders, filled, active, edge_src[owner, column], edge_dst[owner, column]

    def one_part(returned, owner):
        totals = jnp.zeros((PART_ROWS, F), jnp.float32)
        degree = jnp.zeros((PART_ROWS,), jnp.float32)
        for column in range(N_SRC):
            senders, filled, active, sources, targets = column_data(owner, column)
            fetched = blocks[:, column][peer_index[:, None], jnp.maximum(senders, 0)]
            fetched = jnp.where(filled[:, :, None], fetched, jnp.zeros((), jnp.bfloat16))
            table = jnp.concatenate([blocks[owner, column], fetched.reshape(HALO, F)], axis=0)
            gathered = jnp.where(active[:, None], table[sources], jnp.zeros((), jnp.bfloat16))
            partial_value = jnp.zeros((PART_ROWS, F), jnp.float32).at[targets].add(gathered.astype(jnp.float32))
            rounded = lax.optimization_barrier(partial_value.astype(jnp.bfloat16))
            totals = totals + rounded.astype(jnp.float32)
            degree = degree + jnp.zeros((PART_ROWS,), jnp.float32).at[targets].add(active.astype(jnp.float32))
        inverse = 1.0 / jnp.maximum(degree, 1.0)
        neighbour_mean = (totals * inverse[:, None]).astype(jnp.bfloat16)
        own_rows = blocks[owner].reshape(PART_ROWS, F)
        preact = (jnp.dot(own_rows, w_self, preferred_element_type=jnp.float32)
                  + jnp.dot(neighbour_mean, w_neigh, preferred_element_type=jnp.float32)
                  + bias.astype(jnp.float32))
        sigma = jax.nn.sigmoid(preact)
        outputs = (preact * sigma).astype(jnp.bfloat16)
        slope = sigma * (1.0 + preact * (1.0 - sigma))
        upstream = (upstreams[owner].reshape(PART_ROWS, H).astype(jnp.float32) * slope).astype(jnp.bfloat16)
        grad_own = jnp.dot(upstream, w_self.T, preferred_element_type=jnp.float32)
        scaled = (jnp.dot(upstream, w_neigh.T, preferred_element_type=jnp.float32) * inverse[:, None]).astype(jnp.bfloat16)
        grad_parts = []
        for column in range(N_SRC):
            senders, filled, active, sources, targets = column_data(owner, column)
            contrib = jnp.where(active[:, None], scaled[targets], jnp.zeros((), jnp.bfloat16)).astype(jnp.float32)
            grad_table = jnp.zeros((NODE_DEV + HALO, F), jnp.float32).at[sources].add(contrib)
            grad_parts.append(grad_table[:NODE_DEV])
            remote_grad = grad_table[NODE_DEV:].reshape(N_DOM, CAP, F)
            target_rows = jnp.where(filled, senders, NODE_DEV)
            returned = returned.at[peer_index[:, None], column, target_rows].add(remote_grad, mode="drop")
        grad_feat = grad_own + jnp.concatenate(grad_parts, axis=0)
        return returned, (outputs, grad_feat)

    start = jnp.zeros((N_DOM, N_SRC, NODE_DEV, F), jnp.float32)
    returned, (outputs, grad_feat) = lax.scan(one_part, start, jnp.arange(N_DOM))
    total_grad = grad_feat.reshape(N_DOM, N_SRC, NODE_DEV, F) + returned
    return outputs.reshape(NODES, H), total_grad.reshape(NODES, F)
```

```python
import functools

import jax
import jax.numpy as jnp
from jax import lax
from jax.experimental import pallas as pl
from jax.experimental.pallas import tpu as pltpu
from jax.sharding import PartitionSpec as P

MESH = pl.DeviceIdType.MESH
CHUNK = 256
STRIP = 64
F32 = jnp.float32
BF16 = jnp.bfloat16


def build_kernel(width, halves, word_ref, count_ref, feature_ref, sender_ref, adjacency_ref, degree_ref, picked_ref,
                 unit, stage, stage_sem, *tables):
    total_rows = tables[0].shape[0]
    lanes = len(tables)

    row_at = lax.broadcasted_iota(jnp.int32, unit.shape, 0)
    lane_at = lax.broadcasted_iota(jnp.int32, unit.shape, 1)
    unit[...] = jnp.where(
        row_at == lane_at, 1, jnp.where(row_at == lane_at + 128, 65536, 0)
    ).astype(jnp.int32)
    zeros = jnp.zeros((128, 128), jnp.int32)

    def clear(step, carry):
        for table in tables:
            table[pl.ds(pl.multiple_of(step * 128, 128), 128), :] = zeros
        return carry

    lax.fori_loop(0, total_rows // 128, clear, 0)

    def edge_tile(tile, carry):
        base = tile * 128
        for group in range(0, 128, lanes):
            words = [word_ref[base + group + k] for k in range(lanes)]
            rows = [pl.ds(lax.shift_right_logical(word, 8), 1) for word in words]
            sums = [
                tables[k][rows[k], :] + unit[pl.ds(words[k] & 255, 1), :] for k in range(lanes)
            ]
            for k in range(lanes):
                tables[k][rows[k], :] = sums[k]
        return carry

    lax.fori_loop(0, count_ref[0], edge_tile, 0)

    accounts = feature_ref.shape[0]
    slots = sender_ref.shape[1]
    chosen = lax.broadcasted_iota(jnp.int32, (accounts, slots), 0) == sender_ref[...]
    picked_ref[...] = lax.dot_general(
        chosen.astype(F32).astype(BF16), feature_ref[...], (((0,), (0,)), ((), ())), preferred_element_type=F32
    )

    degree_ref[...] = jnp.zeros_like(degree_ref)
    per_block = accounts // CHUNK
    copies = []
    for chunk in range(halves // 2):
        for side in range(2):
            first = (2 * chunk + side) * width
            columns = pl.ds(side * 128, 128)

            def unpack(step, sums, first=first, columns=columns, chunk=chunk):
                rows = pl.ds(pl.multiple_of(first + step * STRIP, STRIP), STRIP)
                packed = tables[0][rows, :]
                for table in tables[1:]:
                    packed = packed + table[rows, :]
                low = (packed & 65535).astype(F32)
                high = lax.shift_right_logical(packed, 16).astype(F32)
                out = pl.ds(pl.multiple_of(step * STRIP, STRIP), STRIP)
                stage[chunk, out, columns] = low.astype(BF16)
                stage[chunk + halves // 2, out, columns] = high.astype(BF16)
                low_sum = jnp.sum(low.reshape(STRIP // 8, 8, 128), axis=0)
                high_sum = jnp.sum(high.reshape(STRIP // 8, 8, 128), axis=0)
                return sums[0] + low_sum, sums[1] + high_sum

            start = jnp.zeros((8, 128), F32)
            low_sum, high_sum = lax.fori_loop(0, width // STRIP, unpack, (start, start))
            for at, value in ((chunk, low_sum), (chunk + halves // 2, high_sum)):
                degree_ref[at // per_block, pl.ds(at % per_block, 1), columns] = jnp.sum(
                    value, axis=0, keepdims=True
                )
        for at in (chunk, chunk + halves // 2):
            copy = pltpu.make_async_copy(stage.at[at], adjacency_ref.at[at], stage_sem.at[at])
            copy.start()
            copies.append(copy)
    for copy in copies:
        copy.wait()


def layer_kernel(doms, adjacency_ref, degree_ref, picked_ref, feature_ref, cotangent_ref, self_ref, neigh_ref,
                 bias_ref, sender_ref, act_ref, grad_ref,
                 adjacency, table_t, halo, halo_t, degree_in, inverse, own_pre,
                 foreign, kept, to_sibling, from_sibling, chip_out, chip_in, own_out, own_in, spread,
                 halo_grad, returned,
                 load_sem, halo_send, halo_recv, degree_send, degree_recv, part_send, part_recv, grad_send, grad_recv,
                 back_send, back_recv):
    part, source = lax.axis_index("dom"), lax.axis_index("src")
    chip, core = source // 2, source % 2
    sibling = chip * 2 + (1 - core)
    opposite = (1 - chip) * 2 + core
    diagonal = (1 - chip) * 2 + (1 - core)
    rows = feature_ref.shape[0]
    per_block = rows // CHUNK
    capacity = halo.shape[0] // doms

    barrier = pltpu.get_barrier_semaphore()
    for step in range(1, 4):
        pl.semaphore_signal(barrier, inc=1, device_id=(part, lax.rem(source + step, 4)), device_id_type=MESH)

    def greet(step, carry):
        pl.semaphore_signal(barrier, inc=1, device_id=(lax.rem(part + step, doms), source), device_id_type=MESH)
        return carry

    lax.fori_loop(1, doms, greet, 0)

    def load(chunk):
        return pltpu.make_async_copy(adjacency_ref.at[chunk], adjacency.at[chunk], load_sem.at[chunk])

    def load_block(block):
        def go(step, carry):
            load(block * per_block + step).start()
            return carry

        lax.fori_loop(0, per_block, go, 0)

    for block in (diagonal, opposite, sibling, source):
        load_block(block)
    table_t[...] = feature_ref[...].astype(F32).T.astype(BF16)
    pl.semaphore_wait(barrier, 3 + doms - 1)

    def slot(at):
        return pl.ds(pl.multiple_of(at * capacity, capacity), capacity)

    def halo_copy(step):
        peer = lax.rem(part + step, doms)
        return pltpu.make_async_remote_copy(
            src_ref=picked_ref.at[slot(peer)], dst_ref=halo.at[slot(part)],
            send_sem=halo_send.at[step], recv_sem=halo_recv.at[step],
            device_id=(peer, source), device_id_type=MESH)

    def back_copy(step):
        peer = lax.rem(part + step, doms)
        return pltpu.make_async_remote_copy(
            src_ref=halo_grad.at[slot(peer)], dst_ref=returned.at[slot(part)],
            send_sem=back_send.at[step], recv_sem=back_recv.at[step],
            device_id=(peer, source), device_id_type=MESH)

    def each_peer(action):
        def go(step, carry):
            action(step)
            return carry

        lax.fori_loop(1, doms, go, 0)

    each_peer(lambda step: halo_copy(step).start())

    def degree_copy(step):
        peer = lax.rem(source + step, 4)
        return pltpu.make_async_remote_copy(
            src_ref=degree_ref.at[peer], dst_ref=degree_in.at[step],
            send_sem=degree_send.at[step], recv_sem=degree_recv.at[step],
            device_id=(part, peer), device_id_type=MESH)

    for step in range(1, 4):
        degree_copy(step).start()

    def part_copy(kind, step):
        source_ref, target_ref, peer = (
            (to_sibling, from_sibling, sibling),
            (chip_out, chip_in, opposite),
            (own_out, own_in, sibling),
        )[kind]
        return pltpu.make_async_remote_copy(
            src_ref=source_ref.at[step], dst_ref=target_ref.at[step],
            send_sem=part_send.at[kind, step], recv_sem=part_recv.at[kind, step],
            device_id=(part, peer), device_id_type=MESH)

    def grad_copy(kind, step):
        owner, peer = ((source, sibling), (source, opposite), (opposite, sibling))[kind]
        at = owner * per_block + step
        return pltpu.make_async_remote_copy(
            src_ref=spread.at[at], dst_ref=spread.at[at],
            send_sem=grad_send.at[kind, step], recv_sem=grad_recv.at[kind, step],
            device_id=(part, peer), device_id_type=MESH)

    def each_chunk(action):
        def go(step, carry):
            action(step)
            return carry

        lax.fori_loop(0, per_block, go, 0)

    def from_local(at):
        return jnp.dot(table_t[...], adjacency[at, 0:rows, :], preferred_element_type=F32)

    def from_halo(at):
        return jnp.dot(halo_t[...], adjacency[at, rows:, :], preferred_element_type=F32)

    def early(step):
        at = diagonal * per_block + step
        load(at).wait()
        foreign[step] = from_local(at)

    def early_kept(step):
        at = opposite * per_block + step
        load(at).wait()
        kept[step] = from_local(at)

    each_chunk(early)
    each_chunk(early_kept)
    halo[slot(part), :] = jnp.zeros((capacity, halo.shape[1]), F32)
    returned[slot(part), :] = jnp.zeros((capacity, halo.shape[1]), F32)
    each_peer(lambda step: halo_copy(step).wait_recv())
    halo_t[...] = halo[...].T.astype(BF16)

    def send_foreign(step):
        to_sibling[step] = (foreign[step] + from_halo(diagonal * per_block + step)).astype(BF16)
        part_copy(0, step).start()

    each_chunk(send_foreign)

    def send_chip(step):
        mine = kept[step] + from_halo(opposite * per_block + step)
        part_copy(0, step).wait_recv()
        chip_out[step] = (mine + from_sibling[step].astype(F32)).astype(BF16)
        part_copy(1, step).start()

    each_chunk(send_chip)

    def send_own(step):
        at = sibling * per_block + step
        load(at).wait()
        own_out[step] = (from_local(at) + from_halo(at)).astype(BF16)
        part_copy(2, step).start()

    each_chunk(send_own)

    def keep_own(step):
        at = source * per_block + step
        load(at).wait()
        foreign[step] = from_local(at) + from_halo(at)

    each_chunk(keep_own)
    own_pre[...] = jnp.dot(feature_ref[...], self_ref[...], preferred_element_type=F32) + bias_ref[...].astype(F32)

    degree = degree_ref[source]
    for step in range(1, 4):
        degree_copy(step).wait_recv()
        degree = degree + degree_in[step]
    inverse[...] = 1.0 / jnp.maximum(degree, 1.0)
    halo_grad[...] = jnp.zeros_like(halo_grad)

    def back_halo(at):
        halo_grad[...] += jnp.dot(adjacency[at, rows:, :], spread[at], preferred_element_type=F32)

    def back_local(at):
        grad_ref[...] += jnp.dot(adjacency[at, 0:rows, :], spread[at], preferred_element_type=F32)

    def dense(step):
        here = pl.ds(pl.multiple_of(step * CHUNK, CHUNK), CHUNK)
        inverse_row = inverse[pl.ds(step, 1), :]
        half = jnp.broadcast_to(inverse_row, (128, CHUNK)).T
        inverse_column = jnp.concatenate([half] * (act_ref.shape[1] // 128), axis=1)
        part_copy(2, step).wait_recv()
        part_copy(1, step).wait_recv()
        total_t = foreign[step] + own_in[step].astype(F32) + chip_in[step].astype(F32)
        mean = (total_t * inverse_row).T.astype(BF16)
        preact = own_pre[here, :] + jnp.dot(mean, neigh_ref[...], preferred_element_type=F32)
        sigma = jax.nn.sigmoid(preact)
        slope = sigma * (1.0 + preact * (1.0 - sigma))
        upstream = (cotangent_ref[here, :].astype(F32) * slope).astype(BF16)
        contract = (((1,), (1,)), ((), ()))
        at = source * per_block + step
        spread[at] = (
            lax.dot_general(upstream, neigh_ref[...], contract, preferred_element_type=F32) * inverse_column
        ).astype(BF16)
        grad_copy(1, step).start()
        grad_copy(0, step).start()
        act_ref[here, :] = (preact * sigma).astype(BF16)
        grad_ref[here, :] = lax.dot_general(upstream, self_ref[...], contract, preferred_element_type=F32)

    each_chunk(dense)

    def back_own(step):
        at = source * per_block + step
        back_halo(at)
        back_local(at)

    def back_sibling(step):
        at = sibling * per_block + step
        grad_copy(0, step).wait_recv()
        back_halo(at)
        back_local(at)

    def back_opposite(step):
        grad_copy(1, step).wait_recv()
        grad_copy(2, step).start()
        at = opposite * per_block + step
        back_halo(at)
        back_local(at)

    def back_diagonal(step):
        grad_copy(2, step).wait_recv()
        back_halo(diagonal * per_block + step)

    each_chunk(back_own)
    each_chunk(back_sibling)
    each_chunk(back_opposite)
    each_chunk(back_diagonal)
    each_peer(lambda step: back_copy(step).start())
    each_chunk(lambda step: back_local(diagonal * per_block + step))

    chosen = lax.broadcasted_iota(jnp.int32, (rows, halo.shape[0]), 0) == sender_ref[...]
    each_peer(lambda step: back_copy(step).wait_recv())
    grad_ref[...] += jnp.dot(
        chosen.astype(F32).astype(BF16), returned[...].astype(BF16), preferred_element_type=F32
    )

    each_peer(lambda step: halo_copy(step).wait_send())
    each_peer(lambda step: back_copy(step).wait_send())
    for step in range(1, 4):
        degree_copy(step).wait_send()
    for kind in range(3):
        each_chunk(lambda step, kind=kind: part_copy(kind, step).wait_send())
        each_chunk(lambda step, kind=kind: grad_copy(kind, step).wait_send())


def local(features, cotangent, w_self, w_neigh, bias, send_rows, edge_src, edge_dst, tile_count):
    rows, features_wide = features.shape
    doms, columns = lax.axis_size("dom"), lax.axis_size("src")
    slots = send_rows.shape[2] * send_rows.shape[3]
    width = rows + slots
    part_rows = rows * columns
    halves = part_rows // 256
    chunks = part_rows // CHUNK
    per_block = rows // CHUNK
    lanes = 4 if width <= 1152 else 2
    vmem = pl.BlockSpec(memory_space=pltpu.VMEM)
    smem = pl.BlockSpec(memory_space=pltpu.SMEM)
    anywhere = pl.BlockSpec(memory_space=pl.ANY)

    target = edge_dst[0, 0]
    half_rows = part_rows // 2
    upper = (target >= half_rows).astype(jnp.int32)
    within = target - upper * half_rows
    words = ((within // 128) * width + edge_src[0, 0]) * 256 + within % 128 + upper * 128
    senders = send_rows.reshape(1, slots)

    adjacency, degree, picked = pl.pallas_call(
        functools.partial(build_kernel, width, halves),
        out_shape=(
            jax.ShapeDtypeStruct((chunks, width, CHUNK), BF16),
            jax.ShapeDtypeStruct((columns, 8, CHUNK), F32),
            jax.ShapeDtypeStruct((slots, features_wide), F32),
        ),
        in_specs=[smem, smem, vmem, vmem],
        out_specs=(anywhere, vmem, vmem),
        scratch_shapes=[
            pltpu.VMEM((256, 128), jnp.int32),
            pltpu.VMEM((chunks, width, CHUNK), BF16),
            pltpu.SemaphoreType.DMA((chunks,)),
        ] + [pltpu.VMEM((halves * width, 128), jnp.int32)] * lanes,
        compiler_params=pltpu.CompilerParams(vmem_limit_bytes=58 * 1024 * 1024),
        name="count_edges",
    )(words, tile_count.reshape(1), features, senders)

    wide = features_wide
    dma = pltpu.SemaphoreType.DMA
    block_half = pltpu.VMEM((per_block, wide, CHUNK), BF16)
    block_full = pltpu.VMEM((per_block, wide, CHUNK), F32)
    return pl.pallas_call(
        functools.partial(layer_kernel, doms),
        out_shape=(
            jax.ShapeDtypeStruct((rows, wide), BF16),
            jax.ShapeDtypeStruct((rows, wide), F32),
        ),
        in_specs=[anywhere] + [vmem] * 8,
        out_specs=(vmem, vmem),
        scratch_shapes=[
            pltpu.VMEM((chunks, width, CHUNK), BF16),
            pltpu.VMEM((wide, rows), BF16),
            pltpu.VMEM((slots, wide), F32),
            pltpu.VMEM((wide, slots), BF16),
            pltpu.VMEM((4, 8, CHUNK), F32),
            pltpu.VMEM((8, CHUNK), F32),
            pltpu.VMEM((rows, wide), F32),
            block_full, block_full,
            block_half, block_half, block_half, block_half, block_half, block_half,
            pltpu.VMEM((chunks, CHUNK, wide), BF16),
            pltpu.VMEM((slots, wide), F32),
            pltpu.VMEM((slots, wide), F32),
            dma((chunks,)),
            dma((doms,)), dma((doms,)),
            dma((4,)), dma((4,)),
            dma((3, per_block)), dma((3, per_block)),
            dma((3, per_block)), dma((3, per_block)),
            dma((doms,)), dma((doms,)),
        ],
        compiler_params=pltpu.CompilerParams(
            collective_id=0, has_side_effects=True, vmem_limit_bytes=58 * 1024 * 1024
        ),
        name="layer",
    )(adjacency, degree, picked, features, cotangent, w_self, w_neigh, bias.reshape(1, wide), senders)


def solution(mesh):
    placed = (
        P(("dom", "src"), None),
        P(("dom", "src"), None),
        P(),
        P(),
        P(),
        P("dom", "src", None, None),
        P("dom", "src", None),
        P("dom", "src", None),
        P("dom", "src"),
    )
    return jax.shard_map(
        local,
        mesh=mesh,
        in_specs=placed,
        out_specs=(P(("dom", "src"), None), P(("dom", "src"), None)),
        check_vma=False,
    )
```

```python
import functools

import jax
import jax.numpy as jnp
from jax import lax
from jax.experimental import pallas as pl
from jax.experimental.pallas import tpu as pltpu
from jax.sharding import PartitionSpec as P

MESH = pl.DeviceIdType.MESH
CHUNK = 256
STRIP = 64
F32 = jnp.float32
BF16 = jnp.bfloat16


def strip_of(width):
    return max(rows for rows in range(16, 321, 16) if width % rows == 0)


def build_kernel(width, word_ref, count_ref, feature_ref, sender_ref, adjacency_ref, degree_ref, picked_ref, row_ref,
                 unit, stage, stage_sem, *tables):
    total_rows = tables[0].shape[0]
    lanes = len(tables)
    accounts = feature_ref.shape[0]
    per_block = accounts // CHUNK
    blocks = stage.shape[0] // per_block
    strip = strip_of(width)
    tiles = count_ref[0]

    row_at = lax.broadcasted_iota(jnp.int32, unit.shape, 0)
    lane_at = lax.broadcasted_iota(jnp.int32, unit.shape, 1)
    unit[...] = sum(
        jnp.where(row_at == lane_at + 128 * field, 1 << (8 * field), 0).astype(jnp.int32) for field in range(4)
    )
    zeros = jnp.zeros((128, 128), jnp.int32)

    def clear(chosen):
        def go(step, carry):
            for table in chosen:
                table[pl.ds(pl.multiple_of(step * 128, 128), 128), :] = zeros
            return carry

        lax.fori_loop(0, total_rows // 128, go, 0)

    clear(tables)

    def edge_tile(tile, carry):
        base = tile * 128
        for group in range(0, 128, lanes):
            words = [word_ref[base + group + k] for k in range(lanes)]
            rows = [pl.ds(lax.shift_right_logical(word, 9), 1) for word in words]
            sums = [
                tables[k][rows[k], :] + unit[pl.ds(words[k] & 511, 1), :] for k in range(lanes)
            ]
            for k in range(lanes):
                tables[k][rows[k], :] = sums[k]
        return carry

    lax.fori_loop(0, tiles, edge_tile, 0)

    peers, capacity = sender_ref.shape[2:]
    slots = peers * capacity
    sender = sender_ref[0, 0]
    repeat = (
        lax.broadcasted_iota(jnp.int32, (capacity, slots), 1) % capacity
        == lax.broadcasted_iota(jnp.int32, (capacity, slots), 0)
    ).astype(F32).astype(BF16)
    high = jnp.dot(lax.shift_right_arithmetic(sender, 5).astype(F32).astype(BF16), repeat, preferred_element_type=F32)
    low = jnp.dot((sender & 31).astype(F32).astype(BF16), repeat, preferred_element_type=F32)
    mine = (
        lax.broadcasted_iota(jnp.int32, (peers, slots), 1) // capacity
        == lax.broadcasted_iota(jnp.int32, (peers, slots), 0)
    )
    row = jnp.sum(jnp.where(mine, high * 32.0 + low, 0.0), axis=0, keepdims=True).astype(jnp.int32)
    row_ref[...] = row
    chosen = lax.broadcasted_iota(jnp.int32, (accounts, slots), 0) == row
    picked_ref[...] = lax.dot_general(
        chosen.astype(F32).astype(BF16), feature_ref[...], (((0,), (0,)), ((), ())), preferred_element_type=F32
    )

    degree_ref[...] = jnp.zeros_like(degree_ref)

    def stage_copy(at):
        return pltpu.make_async_copy(stage.at[at], adjacency_ref.at[at], stage_sem.at[at])

    counted = jnp.zeros((8, 128), F32)
    for piece in range(per_block):
        for side in range(2):
            first = (2 * piece + side) * width
            columns = pl.ds(side * 128, 128)

            def unpack(step, sums, first=first, columns=columns, piece=piece):
                rows = pl.ds(pl.multiple_of(first + step * strip, 16), strip)
                packed = tables[0][rows, :]
                for table in tables[1:]:
                    packed = packed + table[rows, :]
                out = pl.ds(pl.multiple_of(step * strip, 16), strip)
                after = []
                for field in range(4):
                    value = packed if field == 0 else lax.shift_right_logical(packed, 8 * field)
                    value = (value if field == 3 else value & 255).astype(F32)
                    stage[field * per_block + piece, out, columns] = value.astype(BF16)
                    after.append(sums[field] + jnp.sum(value.reshape(strip // 8, 8, 128), axis=0))
                return tuple(after)

            sums = lax.fori_loop(0, width // strip, unpack, (jnp.zeros((8, 128), F32),) * 4)
            for field in range(4):
                degree_ref[field, pl.ds(piece, 1), columns] = jnp.sum(sums[field], axis=0, keepdims=True)
                counted = counted + sums[field]
        for field in range(4):
            stage_copy(field * per_block + piece).start()
    for at in range(blocks * per_block):
        stage_copy(at).wait()

    @pl.when(jnp.sum(counted).astype(jnp.int32) != tiles * 128)
    def _():
        table = tables[0]

        def field_pass(field, carry):
            clear(tables[:1])

            def one(edge, carry):
                word = word_ref[edge]
                match = jnp.where(lax.shift_right_logical(word, 7) % 4 == field, 1, 0)
                rows = pl.ds(lax.shift_right_logical(word, 9), 1)
                table[rows, :] = table[rows, :] + unit[pl.ds(word & 127, 1), :] * match
                return carry

            lax.fori_loop(0, tiles * 128, one, 0)
            for piece in range(per_block):
                for side in range(2):
                    value = table[pl.ds((2 * piece + side) * width, width), :].astype(F32)
                    columns = pl.ds(side * 128, 128)
                    stage[field * per_block + piece, :, columns] = value.astype(BF16)
                    degree_ref[field, pl.ds(piece, 1), columns] = jnp.sum(value, axis=0, keepdims=True)
            return carry

        lax.fori_loop(0, 4, field_pass, 0)
        for at in range(blocks * per_block):
            stage_copy(at).start()
        for at in range(blocks * per_block):
            stage_copy(at).wait()


def layer_kernel(doms, adjacency_ref, degree_ref, picked_ref, feature_ref, cotangent_ref, self_ref, neigh_ref,
                 bias_ref, act_ref, grad_ref, returned_ref,
                 adjacency, table_t, halo, halo_t, degree_in, inverse, own_pre,
                 foreign, kept, to_sibling, from_sibling, chip_out, chip_in, own_out, own_in, spread,
                 halo_grad, returned,
                 load_sem, halo_send, halo_recv, degree_send, degree_recv, part_send, part_recv, grad_send, grad_recv,
                 back_send, back_recv):
    part, source = lax.axis_index("dom"), lax.axis_index("src")
    chip, core = source // 2, source % 2
    sibling = chip * 2 + (1 - core)
    opposite = (1 - chip) * 2 + core
    diagonal = (1 - chip) * 2 + (1 - core)
    rows = feature_ref.shape[0]
    per_block = rows // CHUNK
    capacity = halo.shape[0] // doms

    barrier = pltpu.get_barrier_semaphore()
    for step in range(1, 4):
        pl.semaphore_signal(barrier, inc=1, device_id=(part, lax.rem(source + step, 4)), device_id_type=MESH)

    def greet(step, carry):
        pl.semaphore_signal(barrier, inc=1, device_id=(lax.rem(part + step, doms), source), device_id_type=MESH)
        return carry

    lax.fori_loop(1, doms, greet, 0)

    def load(chunk):
        return pltpu.make_async_copy(adjacency_ref.at[chunk], adjacency.at[chunk], load_sem.at[chunk])

    def load_block(block):
        def go(step, carry):
            load(block * per_block + step).start()
            return carry

        lax.fori_loop(0, per_block, go, 0)

    for block in (diagonal, opposite, sibling, source):
        load_block(block)
    table_t[...] = feature_ref[...].astype(F32).T.astype(BF16)
    pl.semaphore_wait(barrier, 3 + doms - 1)

    def slot(at):
        return pl.ds(pl.multiple_of(at * capacity, capacity), capacity)

    def halo_copy(step):
        peer = lax.rem(part + step, doms)
        return pltpu.make_async_remote_copy(
            src_ref=picked_ref.at[slot(peer)], dst_ref=halo.at[slot(part)],
            send_sem=halo_send.at[step], recv_sem=halo_recv.at[step],
            device_id=(peer, source), device_id_type=MESH)

    def back_copy(step):
        peer = lax.rem(part + step, doms)
        return pltpu.make_async_remote_copy(
            src_ref=halo_grad.at[slot(peer)], dst_ref=returned.at[slot(part)],
            send_sem=back_send.at[step], recv_sem=back_recv.at[step],
            device_id=(peer, source), device_id_type=MESH)

    def each_peer(action):
        def go(step, carry):
            action(step)
            return carry

        lax.fori_loop(1, doms, go, 0)

    each_peer(lambda step: halo_copy(step).start())

    def degree_copy(step):
        peer = lax.rem(source + step, 4)
        return pltpu.make_async_remote_copy(
            src_ref=degree_ref.at[peer], dst_ref=degree_in.at[step],
            send_sem=degree_send.at[step], recv_sem=degree_recv.at[step],
            device_id=(part, peer), device_id_type=MESH)

    for step in range(1, 4):
        degree_copy(step).start()

    def part_copy(kind, step):
        source_ref, target_ref, peer = (
            (to_sibling, from_sibling, sibling),
            (chip_out, chip_in, opposite),
            (own_out, own_in, sibling),
        )[kind]
        return pltpu.make_async_remote_copy(
            src_ref=source_ref.at[step], dst_ref=target_ref.at[step],
            send_sem=part_send.at[kind, step], recv_sem=part_recv.at[kind, step],
            device_id=(part, peer), device_id_type=MESH)

    def grad_copy(kind, step):
        owner, peer = ((source, sibling), (source, opposite), (opposite, sibling))[kind]
        at = owner * per_block + step
        return pltpu.make_async_remote_copy(
            src_ref=spread.at[at], dst_ref=spread.at[at],
            send_sem=grad_send.at[kind, step], recv_sem=grad_recv.at[kind, step],
            device_id=(part, peer), device_id_type=MESH)

    def each_chunk(action):
        def go(step, carry):
            action(step)
            return carry

        lax.fori_loop(0, per_block, go, 0)

    def from_local(at):
        return jnp.dot(table_t[...], adjacency[at, 0:rows, :], preferred_element_type=F32)

    def from_halo(at):
        return jnp.dot(halo_t[...], adjacency[at, rows:, :], preferred_element_type=F32)

    def early(step):
        at = diagonal * per_block + step
        load(at).wait()
        foreign[step] = from_local(at)

    def early_kept(step):
        at = opposite * per_block + step
        load(at).wait()
        kept[step] = from_local(at)

    each_chunk(early)
    each_chunk(early_kept)
    halo[slot(part), :] = jnp.zeros((capacity, halo.shape[1]), F32)
    returned[slot(part), :] = jnp.zeros((capacity, halo.shape[1]), F32)
    each_peer(lambda step: halo_copy(step).wait_recv())
    halo_t[...] = halo[...].T.astype(BF16)

    def send_foreign(step):
        to_sibling[step] = (foreign[step] + from_halo(diagonal * per_block + step)).astype(BF16)
        part_copy(0, step).start()

    each_chunk(send_foreign)

    def send_chip(step):
        mine = kept[step] + from_halo(opposite * per_block + step)
        part_copy(0, step).wait_recv()
        chip_out[step] = (mine + from_sibling[step].astype(F32)).astype(BF16)
        part_copy(1, step).start()

    each_chunk(send_chip)

    def send_own(step):
        at = sibling * per_block + step
        load(at).wait()
        own_out[step] = (from_local(at) + from_halo(at)).astype(BF16)
        part_copy(2, step).start()

    each_chunk(send_own)

    def keep_own(step):
        at = source * per_block + step
        load(at).wait()
        foreign[step] = from_local(at) + from_halo(at)

    each_chunk(keep_own)
    own_pre[...] = jnp.dot(feature_ref[...], self_ref[...], preferred_element_type=F32) + bias_ref[...].astype(F32).reshape(1, -1)

    degree = degree_ref[source]
    for step in range(1, 4):
        degree_copy(step).wait_recv()
        degree = degree + degree_in[step]
    inverse[...] = 1.0 / jnp.maximum(degree, 1.0)
    halo_grad[...] = jnp.zeros_like(halo_grad)

    def back_halo(at):
        halo_grad[...] += jnp.dot(adjacency[at, rows:, :], spread[at], preferred_element_type=F32)

    def back_local(at):
        grad_ref[...] += jnp.dot(adjacency[at, 0:rows, :], spread[at], preferred_element_type=F32)

    def dense(step):
        here = pl.ds(pl.multiple_of(step * CHUNK, CHUNK), CHUNK)
        inverse_row = inverse[pl.ds(step, 1), :]
        half = jnp.broadcast_to(inverse_row, (128, CHUNK)).T
        inverse_column = jnp.concatenate([half] * (act_ref.shape[1] // 128), axis=1)
        part_copy(2, step).wait_recv()
        part_copy(1, step).wait_recv()
        total_t = foreign[step] + own_in[step].astype(F32) + chip_in[step].astype(F32)
        mean = (total_t * inverse_row).T.astype(BF16)
        preact = own_pre[here, :] + jnp.dot(mean, neigh_ref[...], preferred_element_type=F32)
        sigma = jax.nn.sigmoid(preact)
        slope = sigma * (1.0 + preact * (1.0 - sigma))
        upstream = (cotangent_ref[here, :].astype(F32) * slope).astype(BF16)
        contract = (((1,), (1,)), ((), ()))
        at = source * per_block + step
        spread[at] = (
            lax.dot_general(upstream, neigh_ref[...], contract, preferred_element_type=F32) * inverse_column
        ).astype(BF16)
        grad_copy(1, step).start()
        grad_copy(0, step).start()
        act_ref[here, :] = (preact * sigma).astype(BF16)
        grad_ref[here, :] = lax.dot_general(upstream, self_ref[...], contract, preferred_element_type=F32)

    each_chunk(dense)

    def back_own(step):
        at = source * per_block + step
        back_halo(at)
        back_local(at)

    def back_sibling(step):
        at = sibling * per_block + step
        grad_copy(0, step).wait_recv()
        back_halo(at)
        back_local(at)

    def back_opposite(step):
        grad_copy(1, step).wait_recv()
        grad_copy(2, step).start()
        at = opposite * per_block + step
        back_halo(at)
        back_local(at)

    def back_diagonal(step):
        grad_copy(2, step).wait_recv()
        back_halo(diagonal * per_block + step)

    each_chunk(back_own)
    each_chunk(back_sibling)
    each_chunk(back_opposite)
    each_chunk(back_diagonal)
    each_peer(lambda step: back_copy(step).start())
    each_chunk(lambda step: back_local(diagonal * per_block + step))

    each_peer(lambda step: back_copy(step).wait_recv())
    returned_ref[...] = returned[...]
    each_peer(lambda step: halo_copy(step).wait_send())
    each_peer(lambda step: back_copy(step).wait_send())
    for step in range(1, 4):
        degree_copy(step).wait_send()
    for kind in range(3):
        each_chunk(lambda step, kind=kind: part_copy(kind, step).wait_send())
        each_chunk(lambda step, kind=kind: grad_copy(kind, step).wait_send())


def finish_kernel(part_act_ref, part_grad_ref, returned_ref, row_ref, act_ref, grad_ref):
    first = pl.program_id(0) * act_ref.shape[0]
    chosen = lax.broadcasted_iota(jnp.int32, (act_ref.shape[0], row_ref.shape[1]), 0) + first == row_ref[...]
    act_ref[...] = part_act_ref[...]
    grad_ref[...] = part_grad_ref[...] + jnp.dot(
        chosen.astype(F32).astype(BF16), returned_ref[...].astype(BF16), preferred_element_type=F32
    )


def local(features, cotangent, w_self, w_neigh, bias, send_rows, edge_src, edge_dst, tile_count):
    rows, features_wide = features.shape
    doms, columns = lax.axis_size("dom"), lax.axis_size("src")
    slots = send_rows.shape[2] * send_rows.shape[3]
    width = rows + slots
    chunks = rows * columns // CHUNK
    per_block = rows // CHUNK
    vmem = pl.BlockSpec(memory_space=pltpu.VMEM)
    smem = pl.BlockSpec(memory_space=pltpu.SMEM)
    anywhere = pl.BlockSpec(memory_space=pl.ANY)

    target = edge_dst[0, 0]
    within = target % rows
    words = ((within // 128) * width + edge_src[0, 0]) * 512 + (target // rows) * 128 + within % 128

    adjacency, degree, picked, row = pl.pallas_call(
        functools.partial(build_kernel, width),
        out_shape=(
            jax.ShapeDtypeStruct((chunks, width, CHUNK), BF16),
            jax.ShapeDtypeStruct((columns, 8, CHUNK), F32),
            jax.ShapeDtypeStruct((slots, features_wide), F32),
            jax.ShapeDtypeStruct((1, slots), jnp.int32),
        ),
        in_specs=[smem, smem, vmem, vmem],
        out_specs=(anywhere, vmem, vmem, vmem),
        scratch_shapes=[
            pltpu.VMEM((512, 128), jnp.int32),
            pltpu.VMEM((chunks, width, CHUNK), BF16),
            pltpu.SemaphoreType.DMA((chunks,)),
        ] + [pltpu.VMEM((rows // 128 * width, 128), jnp.int32)] * 4,
        compiler_params=pltpu.CompilerParams(vmem_limit_bytes=58 * 1024 * 1024),
        name="count_edges",
    )(words, tile_count.reshape(1), features, send_rows)

    wide = features_wide
    dma = pltpu.SemaphoreType.DMA
    block_half = pltpu.VMEM((per_block, wide, CHUNK), BF16)
    block_full = pltpu.VMEM((per_block, wide, CHUNK), F32)
    part_act, part_grad, returned = pl.pallas_call(
        functools.partial(layer_kernel, doms),
        out_shape=(
            jax.ShapeDtypeStruct((rows, wide), BF16),
            jax.ShapeDtypeStruct((rows, wide), F32),
            jax.ShapeDtypeStruct((slots, wide), F32),
        ),
        in_specs=[anywhere] + [vmem] * 7,
        out_specs=(vmem, vmem, vmem),
        scratch_shapes=[
            pltpu.VMEM((chunks, width, CHUNK), BF16),
            pltpu.VMEM((wide, rows), BF16),
            pltpu.VMEM((slots, wide), F32),
            pltpu.VMEM((wide, slots), BF16),
            pltpu.VMEM((4, 8, CHUNK), F32),
            pltpu.VMEM((8, CHUNK), F32),
            pltpu.VMEM((rows, wide), F32),
            block_full, block_full,
            block_half, block_half, block_half, block_half, block_half, block_half,
            pltpu.VMEM((chunks, CHUNK, wide), BF16),
            pltpu.VMEM((slots, wide), F32),
            pltpu.VMEM((slots, wide), F32),
            dma((chunks,)),
            dma((doms,)), dma((doms,)),
            dma((4,)), dma((4,)),
            dma((3, per_block)), dma((3, per_block)),
            dma((3, per_block)), dma((3, per_block)),
            dma((doms,)), dma((doms,)),
        ],
        compiler_params=pltpu.CompilerParams(
            collective_id=0, has_side_effects=True, vmem_limit_bytes=58 * 1024 * 1024
        ),
        name="layer",
    )(adjacency, degree, picked, features, cotangent, w_self, w_neigh, bias)

    def band():
        return pl.BlockSpec((CHUNK, wide), lambda step: (step, 0))

    def whole(array):
        return pl.BlockSpec(array.shape, lambda step: (0, 0))

    return pl.pallas_call(
        finish_kernel,
        grid=(rows // CHUNK,),
        out_shape=(
            jax.ShapeDtypeStruct((rows, wide), BF16),
            jax.ShapeDtypeStruct((rows, wide), F32),
        ),
        in_specs=[band(), band(), whole(returned), whole(row)],
        out_specs=(band(), band()),
        compiler_params=pltpu.CompilerParams(vmem_limit_bytes=32 * 1024 * 1024),
        name="finish",
    )(part_act, part_grad, returned, row)


def solution(mesh):
    placed = (
        P(("dom", "src"), None),
        P(("dom", "src"), None),
        P(),
        P(),
        P(),
        P("dom", "src", None, None),
        P("dom", "src", None),
        P("dom", "src", None),
        P("dom", "src"),
    )
    return jax.shard_map(
        local,
        mesh=mesh,
        in_specs=placed,
        out_specs=(P(("dom", "src"), None), P(("dom", "src"), None)),
        check_vma=False,
    )
```

```python
import functools

import jax
import jax.numpy as jnp
from jax import lax
from jax.experimental import pallas as pl
from jax.experimental.pallas import tpu as pltpu
from jax.sharding import PartitionSpec as P

MESH = pl.DeviceIdType.MESH
CHUNK = 256
STRIP = 64
F32 = jnp.float32
BF16 = jnp.bfloat16


def strip_of(width):
    return max(rows for rows in range(16, 321, 16) if width % rows == 0)


def build_kernel(width, source_hbm, target_hbm, feature_hbm, count_ref, sender_ref,
                 adjacency_ref, degree_ref, picked_ref, row_ref,
                 source_ref, target_ref, feature_ref, word_vmem, word_ref, unit, stage, in_sem, stage_sem, *tables):
    incoming = [
        pltpu.make_async_copy(source_hbm.at[0], source_ref, in_sem.at[0]),
        pltpu.make_async_copy(target_hbm.at[0], target_ref, in_sem.at[1]),
        pltpu.make_async_copy(feature_hbm, feature_ref, in_sem.at[2]),
    ]
    for copy in incoming:
        copy.start()
    total_rows = tables[0].shape[0]
    lanes = len(tables)
    accounts = feature_ref.shape[0]
    per_block = accounts // CHUNK
    blocks = stage.shape[0] // per_block
    strip = strip_of(width)
    tiles = count_ref[0]

    incoming[0].wait()
    incoming[1].wait()
    target = target_ref[...]
    within = target % accounts
    word_vmem[...] = ((within // 128) * width + source_ref[...]) * 512 + (target // accounts) * 128 + within % 128
    word_copy = pltpu.make_async_copy(word_vmem, word_ref, in_sem.at[3])
    word_copy.start()

    row_at = lax.broadcasted_iota(jnp.int32, unit.shape, 0)
    lane_at = lax.broadcasted_iota(jnp.int32, unit.shape, 1)
    unit[...] = sum(
        jnp.where(row_at == lane_at + 128 * field, 1 << (8 * field), 0).astype(jnp.int32) for field in range(4)
    )
    zeros = jnp.zeros((128, 128), jnp.int32)

    def clear(chosen):
        def go(step, carry):
            for table in chosen:
                table[pl.ds(pl.multiple_of(step * 128, 128), 128), :] = zeros
            return carry

        lax.fori_loop(0, total_rows // 128, go, 0)

    clear(tables)
    word_copy.wait()
    incoming[2].wait()

    def edge_tile(tile, carry):
        base = tile * 128
        for group in range(0, 128, lanes):
            words = [word_ref[0, base + group + k] for k in range(lanes)]
            rows = [pl.ds(lax.shift_right_logical(word, 9), 1) for word in words]
            sums = [
                tables[k][rows[k], :] + unit[pl.ds(words[k] & 511, 1), :] for k in range(lanes)
            ]
            for k in range(lanes):
                tables[k][rows[k], :] = sums[k]
        return carry

    lax.fori_loop(0, tiles, edge_tile, 0)

    peers, capacity = sender_ref.shape[2:]
    slots = peers * capacity
    sender = sender_ref[0, 0]
    repeat = (
        lax.broadcasted_iota(jnp.int32, (capacity, slots), 1) % capacity
        == lax.broadcasted_iota(jnp.int32, (capacity, slots), 0)
    ).astype(F32).astype(BF16)
    high = jnp.dot(lax.shift_right_arithmetic(sender, 5).astype(F32).astype(BF16), repeat, preferred_element_type=F32)
    low = jnp.dot((sender & 31).astype(F32).astype(BF16), repeat, preferred_element_type=F32)
    mine = (
        lax.broadcasted_iota(jnp.int32, (peers, slots), 1) // capacity
        == lax.broadcasted_iota(jnp.int32, (peers, slots), 0)
    )
    row = jnp.sum(jnp.where(mine, high * 32.0 + low, 0.0), axis=0, keepdims=True).astype(jnp.int32)
    row_ref[...] = row
    chosen = lax.broadcasted_iota(jnp.int32, (accounts, slots), 0) == row
    picked_ref[...] = lax.dot_general(
        chosen.astype(F32).astype(BF16), feature_ref[...], (((0,), (0,)), ((), ())), preferred_element_type=F32
    )

    degree_ref[...] = jnp.zeros_like(degree_ref)

    def stage_copy(at):
        return pltpu.make_async_copy(stage.at[at], adjacency_ref.at[at], stage_sem.at[at])

    counted = jnp.zeros((8, 128), F32)
    for piece in range(per_block):
        for side in range(2):
            first = (2 * piece + side) * width
            columns = pl.ds(side * 128, 128)

            def unpack(step, sums, first=first, columns=columns, piece=piece):
                rows = pl.ds(pl.multiple_of(first + step * strip, 16), strip)
                packed = tables[0][rows, :]
                for table in tables[1:]:
                    packed = packed + table[rows, :]
                out = pl.ds(pl.multiple_of(step * strip, 16), strip)
                after = []
                for field in range(4):
                    value = packed if field == 0 else lax.shift_right_logical(packed, 8 * field)
                    value = (value if field == 3 else value & 255).astype(F32)
                    stage[field * per_block + piece, out, columns] = value.astype(BF16)
                    after.append(sums[field] + jnp.sum(value.reshape(strip // 8, 8, 128), axis=0))
                return tuple(after)

            sums = lax.fori_loop(0, width // strip, unpack, (jnp.zeros((8, 128), F32),) * 4)
            for field in range(4):
                degree_ref[field, pl.ds(piece, 1), columns] = jnp.sum(sums[field], axis=0, keepdims=True)
                counted = counted + sums[field]
        for field in range(4):
            stage_copy(field * per_block + piece).start()
    for at in range(blocks * per_block):
        stage_copy(at).wait()

    @pl.when(jnp.sum(counted).astype(jnp.int32) != tiles * 128)
    def _():
        table = tables[0]

        def field_pass(field, carry):
            clear(tables[:1])

            def one(edge, carry):
                word = word_ref[0, edge]
                match = jnp.where(lax.shift_right_logical(word, 7) % 4 == field, 1, 0)
                rows = pl.ds(lax.shift_right_logical(word, 9), 1)
                table[rows, :] = table[rows, :] + unit[pl.ds(word & 127, 1), :] * match
                return carry

            lax.fori_loop(0, tiles * 128, one, 0)
            for piece in range(per_block):
                for side in range(2):
                    value = table[pl.ds((2 * piece + side) * width, width), :].astype(F32)
                    columns = pl.ds(side * 128, 128)
                    stage[field * per_block + piece, :, columns] = value.astype(BF16)
                    degree_ref[field, pl.ds(piece, 1), columns] = jnp.sum(value, axis=0, keepdims=True)
            return carry

        lax.fori_loop(0, 4, field_pass, 0)
        for at in range(blocks * per_block):
            stage_copy(at).start()
        for at in range(blocks * per_block):
            stage_copy(at).wait()


def layer_kernel(doms, adjacency_ref, degree_ref, picked_ref, feature_hbm, cotangent_hbm, self_hbm, neigh_hbm,
                 bias_hbm, act_hbm, grad_hbm, returned_hbm,
                 feature_ref, cotangent_ref, self_ref, neigh_ref, bias_ref, act_ref, grad_ref,
                 adjacency, table_t, halo, halo_t, degree_in, inverse, own_pre,
                 foreign, kept, to_sibling, from_sibling, chip_out, chip_in, own_out, own_in, spread,
                 halo_grad, returned,
                 in_sem, out_sem, load_sem, halo_send, halo_recv, degree_send, degree_recv, part_send, part_recv, grad_send, grad_recv,
                 back_send, back_recv):
    part, source = lax.axis_index("dom"), lax.axis_index("src")
    chip, core = source // 2, source % 2
    sibling = chip * 2 + (1 - core)
    opposite = (1 - chip) * 2 + core
    diagonal = (1 - chip) * 2 + (1 - core)
    rows = feature_ref.shape[0]
    per_block = rows // CHUNK
    capacity = halo.shape[0] // doms

    barrier = pltpu.get_barrier_semaphore()
    for step in range(1, 4):
        pl.semaphore_signal(barrier, inc=1, device_id=(part, lax.rem(source + step, 4)), device_id_type=MESH)

    def greet(step, carry):
        pl.semaphore_signal(barrier, inc=1, device_id=(lax.rem(part + step, doms), source), device_id_type=MESH)
        return carry

    lax.fori_loop(1, doms, greet, 0)

    def load(chunk):
        return pltpu.make_async_copy(adjacency_ref.at[chunk], adjacency.at[chunk], load_sem.at[chunk])

    def load_block(block):
        def go(step, carry):
            load(block * per_block + step).start()
            return carry

        lax.fori_loop(0, per_block, go, 0)

    incoming = [
        pltpu.make_async_copy(whole, here, in_sem.at[at])
        for at, (whole, here) in enumerate((
            (feature_hbm, feature_ref), (self_hbm, self_ref), (neigh_hbm, neigh_ref), (bias_hbm, bias_ref),
            (cotangent_hbm, cotangent_ref), (degree_ref.at[source], degree_in.at[0]),
        ))
    ]
    incoming[0].start()
    load_block(diagonal)
    load_block(opposite)
    for copy in incoming[1:]:
        copy.start()
    load_block(sibling)
    load_block(source)
    incoming[0].wait()
    table_t[...] = feature_ref[...].astype(F32).T.astype(BF16)
    pl.semaphore_wait(barrier, 3 + doms - 1)

    def slot(at):
        return pl.ds(pl.multiple_of(at * capacity, capacity), capacity)

    def halo_copy(step):
        peer = lax.rem(part + step, doms)
        return pltpu.make_async_remote_copy(
            src_ref=picked_ref.at[slot(peer)], dst_ref=halo.at[slot(part)],
            send_sem=halo_send.at[step], recv_sem=halo_recv.at[step],
            device_id=(peer, source), device_id_type=MESH)

    def back_copy(step):
        peer = lax.rem(part + step, doms)
        return pltpu.make_async_remote_copy(
            src_ref=halo_grad.at[slot(peer)], dst_ref=returned.at[slot(part)],
            send_sem=back_send.at[step], recv_sem=back_recv.at[step],
            device_id=(peer, source), device_id_type=MESH)

    def each_peer(action):
        def go(step, carry):
            action(step)
            return carry

        lax.fori_loop(1, doms, go, 0)

    each_peer(lambda step: halo_copy(step).start())

    def degree_copy(step):
        peer = lax.rem(source + step, 4)
        return pltpu.make_async_remote_copy(
            src_ref=degree_ref.at[peer], dst_ref=degree_in.at[step],
            send_sem=degree_send.at[step], recv_sem=degree_recv.at[step],
            device_id=(part, peer), device_id_type=MESH)

    for step in range(1, 4):
        degree_copy(step).start()

    def part_copy(kind, step):
        source_ref, target_ref, peer = (
            (to_sibling, from_sibling, sibling),
            (chip_out, chip_in, opposite),
            (own_out, own_in, sibling),
        )[kind]
        return pltpu.make_async_remote_copy(
            src_ref=source_ref.at[step], dst_ref=target_ref.at[step],
            send_sem=part_send.at[kind, step], recv_sem=part_recv.at[kind, step],
            device_id=(part, peer), device_id_type=MESH)

    def grad_copy(kind, step):
        owner, peer = ((source, sibling), (source, opposite), (opposite, sibling))[kind]
        at = owner * per_block + step
        return pltpu.make_async_remote_copy(
            src_ref=spread.at[at], dst_ref=spread.at[at],
            send_sem=grad_send.at[kind, step], recv_sem=grad_recv.at[kind, step],
            device_id=(part, peer), device_id_type=MESH)

    def each_chunk(action):
        def go(step, carry):
            action(step)
            return carry

        lax.fori_loop(0, per_block, go, 0)

    def from_local(at):
        return jnp.dot(table_t[...], adjacency[at, 0:rows, :], preferred_element_type=F32)

    def from_halo(at):
        return jnp.dot(halo_t[...], adjacency[at, rows:, :], preferred_element_type=F32)

    def early(step):
        at = diagonal * per_block + step
        load(at).wait()
        foreign[step] = from_local(at)

    def early_kept(step):
        at = opposite * per_block + step
        load(at).wait()
        kept[step] = from_local(at)

    each_chunk(early)
    each_chunk(early_kept)
    halo[slot(part), :] = jnp.zeros((capacity, halo.shape[1]), F32)
    returned[slot(part), :] = jnp.zeros((capacity, halo.shape[1]), F32)
    each_peer(lambda step: halo_copy(step).wait_recv())
    halo_t[...] = halo[...].T.astype(BF16)

    def send_foreign(step):
        to_sibling[step] = (foreign[step] + from_halo(diagonal * per_block + step)).astype(BF16)
        part_copy(0, step).start()

    each_chunk(send_foreign)

    def send_chip(step):
        mine = kept[step] + from_halo(opposite * per_block + step)
        part_copy(0, step).wait_recv()
        chip_out[step] = (mine + from_sibling[step].astype(F32)).astype(BF16)
        part_copy(1, step).start()

    each_chunk(send_chip)

    def send_own(step):
        at = sibling * per_block + step
        load(at).wait()
        own_out[step] = (from_local(at) + from_halo(at)).astype(BF16)
        part_copy(2, step).start()

    each_chunk(send_own)

    def keep_own(step):
        at = source * per_block + step
        load(at).wait()
        foreign[step] = from_local(at) + from_halo(at)

    each_chunk(keep_own)
    for copy in incoming[1:]:
        copy.wait()
    own_pre[...] = jnp.dot(feature_ref[...], self_ref[...], preferred_element_type=F32) + bias_ref[...].astype(F32).reshape(1, -1)

    degree = degree_in[0]
    for step in range(1, 4):
        degree_copy(step).wait_recv()
        degree = degree + degree_in[step]
    inverse[...] = 1.0 / jnp.maximum(degree, 1.0)
    halo_grad[...] = jnp.zeros_like(halo_grad)

    def back_halo(at):
        halo_grad[...] += jnp.dot(adjacency[at, rows:, :], spread[at], preferred_element_type=F32)

    def back_local(at):
        grad_ref[...] += jnp.dot(adjacency[at, 0:rows, :], spread[at], preferred_element_type=F32)

    def act_copy(step):
        here = pl.ds(pl.multiple_of(step * CHUNK, CHUNK), CHUNK)
        return pltpu.make_async_copy(act_ref.at[here], act_hbm.at[here], out_sem.at[step])

    def dense(step):
        here = pl.ds(pl.multiple_of(step * CHUNK, CHUNK), CHUNK)
        inverse_row = inverse[pl.ds(step, 1), :]
        half = jnp.broadcast_to(inverse_row, (128, CHUNK)).T
        inverse_column = jnp.concatenate([half] * (act_ref.shape[1] // 128), axis=1)
        part_copy(2, step).wait_recv()
        part_copy(1, step).wait_recv()
        total_t = foreign[step] + own_in[step].astype(F32) + chip_in[step].astype(F32)
        mean = (total_t * inverse_row).T.astype(BF16)
        preact = own_pre[here, :] + jnp.dot(mean, neigh_ref[...], preferred_element_type=F32)
        sigma = jax.nn.sigmoid(preact)
        slope = sigma * (1.0 + preact * (1.0 - sigma))
        upstream = (cotangent_ref[here, :].astype(F32) * slope).astype(BF16)
        contract = (((1,), (1,)), ((), ()))
        at = source * per_block + step
        spread[at] = (
            lax.dot_general(upstream, neigh_ref[...], contract, preferred_element_type=F32) * inverse_column
        ).astype(BF16)
        grad_copy(1, step).start()
        grad_copy(0, step).start()
        act_ref[here, :] = (preact * sigma).astype(BF16)
        act_copy(step).start()
        grad_ref[here, :] = lax.dot_general(upstream, self_ref[...], contract, preferred_element_type=F32)

    each_chunk(dense)

    def back_own(step):
        at = source * per_block + step
        back_halo(at)
        back_local(at)

    def back_sibling(step):
        at = sibling * per_block + step
        grad_copy(0, step).wait_recv()
        back_halo(at)
        back_local(at)

    def back_opposite(step):
        grad_copy(1, step).wait_recv()
        grad_copy(2, step).start()
        at = opposite * per_block + step
        back_halo(at)
        back_local(at)

    def back_diagonal(step):
        grad_copy(2, step).wait_recv()
        back_halo(diagonal * per_block + step)

    each_chunk(back_own)
    each_chunk(back_sibling)
    each_chunk(back_opposite)
    each_chunk(back_diagonal)
    each_peer(lambda step: back_copy(step).start())
    each_chunk(lambda step: back_local(diagonal * per_block + step))

    grad_out = pltpu.make_async_copy(grad_ref, grad_hbm, out_sem.at[per_block])
    grad_out.start()
    each_peer(lambda step: back_copy(step).wait_recv())
    returned_out = pltpu.make_async_copy(returned, returned_hbm, out_sem.at[per_block + 1])
    returned_out.start()
    each_peer(lambda step: halo_copy(step).wait_send())
    each_peer(lambda step: back_copy(step).wait_send())
    for step in range(1, 4):
        degree_copy(step).wait_send()
    each_chunk(lambda step: act_copy(step).wait())
    for kind in range(3):
        each_chunk(lambda step, kind=kind: part_copy(kind, step).wait_send())
        each_chunk(lambda step, kind=kind: grad_copy(kind, step).wait_send())
    grad_out.wait()
    returned_out.wait()


def finish_kernel(part_act_ref, part_grad_ref, returned_ref, row_ref, act_ref, grad_ref):
    first = pl.program_id(0) * act_ref.shape[0]
    chosen = lax.broadcasted_iota(jnp.int32, (act_ref.shape[0], row_ref.shape[1]), 0) + first == row_ref[...]
    act_ref[...] = part_act_ref[...]
    grad_ref[...] = part_grad_ref[...] + jnp.dot(
        chosen.astype(F32).astype(BF16), returned_ref[...].astype(BF16), preferred_element_type=F32
    )


def local(features, cotangent, w_self, w_neigh, bias, send_rows, edge_src, edge_dst, tile_count):
    rows, features_wide = features.shape
    doms, columns = lax.axis_size("dom"), lax.axis_size("src")
    slots = send_rows.shape[2] * send_rows.shape[3]
    width = rows + slots
    chunks = rows * columns // CHUNK
    per_block = rows // CHUNK
    edges = edge_src.shape[2]
    vmem = pl.BlockSpec(memory_space=pltpu.VMEM)
    smem = pl.BlockSpec(memory_space=pltpu.SMEM)
    anywhere = pl.BlockSpec(memory_space=pl.ANY)

    adjacency, degree, picked, row = pl.pallas_call(
        functools.partial(build_kernel, width),
        out_shape=(
            jax.ShapeDtypeStruct((chunks, width, CHUNK), BF16),
            jax.ShapeDtypeStruct((columns, 8, CHUNK), F32),
            jax.ShapeDtypeStruct((slots, features_wide), F32),
            jax.ShapeDtypeStruct((1, slots), jnp.int32),
        ),
        in_specs=[anywhere, anywhere, anywhere, smem, vmem],
        out_specs=(anywhere, vmem, vmem, vmem),
        scratch_shapes=[
            pltpu.VMEM((1, edges), jnp.int32),
            pltpu.VMEM((1, edges), jnp.int32),
            pltpu.VMEM((rows, features_wide), BF16),
            pltpu.VMEM((1, edges), jnp.int32),
            pltpu.SMEM((1, edges), jnp.int32),
            pltpu.VMEM((512, 128), jnp.int32),
            pltpu.VMEM((chunks, width, CHUNK), BF16),
            pltpu.SemaphoreType.DMA((4,)),
            pltpu.SemaphoreType.DMA((chunks,)),
        ] + [pltpu.VMEM((rows // 128 * width, 128), jnp.int32)] * 4,
        compiler_params=pltpu.CompilerParams(vmem_limit_bytes=58 * 1024 * 1024),
        name="count_edges",
    )(edge_src, edge_dst, features, tile_count.reshape(1), send_rows)

    wide = features_wide
    dma = pltpu.SemaphoreType.DMA
    block_half = pltpu.VMEM((per_block, wide, CHUNK), BF16)
    block_full = pltpu.VMEM((per_block, wide, CHUNK), F32)
    part_act, part_grad, returned = pl.pallas_call(
        functools.partial(layer_kernel, doms),
        out_shape=(
            jax.ShapeDtypeStruct((rows, wide), BF16),
            jax.ShapeDtypeStruct((rows, wide), F32),
            jax.ShapeDtypeStruct((slots, wide), F32),
        ),
        in_specs=[anywhere] * 8,
        out_specs=(anywhere, anywhere, anywhere),
        scratch_shapes=[
            pltpu.VMEM((rows, wide), BF16),
            pltpu.VMEM((rows, wide), BF16),
            pltpu.VMEM(w_self.shape, BF16),
            pltpu.VMEM(w_neigh.shape, BF16),
            pltpu.VMEM(bias.shape, BF16),
            pltpu.VMEM((rows, wide), BF16),
            pltpu.VMEM((rows, wide), F32),
            pltpu.VMEM((chunks, width, CHUNK), BF16),
            pltpu.VMEM((wide, rows), BF16),
            pltpu.VMEM((slots, wide), F32),
            pltpu.VMEM((wide, slots), BF16),
            pltpu.VMEM((4, 8, CHUNK), F32),
            pltpu.VMEM((8, CHUNK), F32),
            pltpu.VMEM((rows, wide), F32),
            block_full, block_full,
            block_half, block_half, block_half, block_half, block_half, block_half,
            pltpu.VMEM((chunks, CHUNK, wide), BF16),
            pltpu.VMEM((slots, wide), F32),
            pltpu.VMEM((slots, wide), F32),
            dma((6,)), dma((per_block + 2,)), dma((chunks,)),
            dma((doms,)), dma((doms,)),
            dma((4,)), dma((4,)),
            dma((3, per_block)), dma((3, per_block)),
            dma((3, per_block)), dma((3, per_block)),
            dma((doms,)), dma((doms,)),
        ],
        compiler_params=pltpu.CompilerParams(
            collective_id=0, has_side_effects=True, vmem_limit_bytes=58 * 1024 * 1024
        ),
        name="layer",
    )(adjacency, degree, picked, features, cotangent, w_self, w_neigh, bias)

    def band():
        return pl.BlockSpec((CHUNK, wide), lambda step: (step, 0))

    def whole(array):
        return pl.BlockSpec(array.shape, lambda step: (0, 0))

    return pl.pallas_call(
        finish_kernel,
        grid=(rows // CHUNK,),
        out_shape=(
            jax.ShapeDtypeStruct((rows, wide), BF16),
            jax.ShapeDtypeStruct((rows, wide), F32),
        ),
        in_specs=[band(), band(), whole(returned), whole(row)],
        out_specs=(band(), band()),
        compiler_params=pltpu.CompilerParams(vmem_limit_bytes=58 * 1024 * 1024),
        name="finish",
    )(part_act, part_grad, returned, row)


def solution(mesh):
    placed = (
        P(("dom", "src"), None),
        P(("dom", "src"), None),
        P(),
        P(),
        P(),
        P("dom", "src", None, None),
        P("dom", "src", None),
        P("dom", "src", None),
        P("dom", "src"),
    )
    return jax.shard_map(
        local,
        mesh=mesh,
        in_specs=placed,
        out_specs=(P(("dom", "src"), None), P(("dom", "src"), None)),
        check_vma=False,
    )
```

```python
import functools

import jax
import jax.numpy as jnp
from jax import lax
from jax.experimental import pallas as pl
from jax.experimental.pallas import tpu as pltpu
from jax.sharding import PartitionSpec as P

MESH = pl.DeviceIdType.MESH
CHUNK = 256
STRIP = 64
F32 = jnp.float32
BF16 = jnp.bfloat16


def strip_of(width):
    return max(rows for rows in range(16, 321, 16) if width % rows == 0)


def build_kernel(width, source_hbm, target_hbm, feature_hbm, count_ref, sender_ref,
                 adjacency_ref, degree_ref, picked_ref, row_ref,
                 source_ref, target_ref, feature_ref, word_vmem, word_ref, unit, stage, in_sem, stage_sem, *tables):
    incoming = [
        pltpu.make_async_copy(source_hbm.at[0], source_ref, in_sem.at[0]),
        pltpu.make_async_copy(target_hbm.at[0], target_ref, in_sem.at[1]),
        pltpu.make_async_copy(feature_hbm, feature_ref, in_sem.at[2]),
    ]
    for copy in incoming:
        copy.start()
    total_rows = tables[0].shape[0]
    lanes = len(tables)
    accounts = feature_ref.shape[0]
    per_block = accounts // CHUNK
    blocks = stage.shape[0] // per_block
    strip = strip_of(width)
    tiles = count_ref[0]

    incoming[0].wait()
    incoming[1].wait()
    target = target_ref[...]
    within = target % accounts
    word_vmem[...] = ((within // 128) * width + source_ref[...]) * 512 + (target // accounts) * 128 + within % 128
    word_copy = pltpu.make_async_copy(word_vmem, word_ref, in_sem.at[3])
    word_copy.start()

    row_at = lax.broadcasted_iota(jnp.int32, unit.shape, 0)
    lane_at = lax.broadcasted_iota(jnp.int32, unit.shape, 1)
    unit[...] = sum(
        jnp.where(row_at == lane_at + 128 * field, 1 << (8 * field), 0).astype(jnp.int32) for field in range(4)
    )
    zeros = jnp.zeros((128, 128), jnp.int32)

    def clear(chosen):
        def go(step, carry):
            for table in chosen:
                table[pl.ds(pl.multiple_of(step * 128, 128), 128), :] = zeros
            return carry

        lax.fori_loop(0, total_rows // 128, go, 0)

    clear(tables)
    word_copy.wait()
    incoming[2].wait()

    def edge_tile(tile, carry):
        base = tile * 128
        for group in range(0, 128, 2 * lanes):
            words = [word_ref[0, base + group + k] for k in range(2 * lanes)]
            rows = [lax.shift_right_logical(word, 9) for word in words]
            units = [word & 511 for word in words]
            sums = []
            for k in range(lanes):
                again = jnp.where(rows[k] == rows[k + lanes], units[k], 512)
                first = unit[pl.ds(units[k], 1), :]
                second = unit[pl.ds(units[k + lanes], 1), :] + unit[pl.ds(again, 1), :]
                sums.append((tables[k][pl.ds(rows[k], 1), :] + first, tables[k][pl.ds(rows[k + lanes], 1), :] + second))
            for k in range(lanes):
                tables[k][pl.ds(rows[k], 1), :] = sums[k][0]
                tables[k][pl.ds(rows[k + lanes], 1), :] = sums[k][1]
        return carry

    lax.fori_loop(0, tiles, edge_tile, 0)

    peers, capacity = sender_ref.shape[2:]
    slots = peers * capacity
    sender = sender_ref[0, 0]
    repeat = (
        lax.broadcasted_iota(jnp.int32, (capacity, slots), 1) % capacity
        == lax.broadcasted_iota(jnp.int32, (capacity, slots), 0)
    ).astype(F32).astype(BF16)
    high = jnp.dot(lax.shift_right_arithmetic(sender, 5).astype(F32).astype(BF16), repeat, preferred_element_type=F32)
    low = jnp.dot((sender & 31).astype(F32).astype(BF16), repeat, preferred_element_type=F32)
    mine = (
        lax.broadcasted_iota(jnp.int32, (peers, slots), 1) // capacity
        == lax.broadcasted_iota(jnp.int32, (peers, slots), 0)
    )
    row = jnp.sum(jnp.where(mine, high * 32.0 + low, 0.0), axis=0, keepdims=True).astype(jnp.int32)
    row_ref[...] = row
    chosen = lax.broadcasted_iota(jnp.int32, (accounts, slots), 0) == row
    picked_ref[...] = lax.dot_general(
        chosen.astype(F32).astype(BF16), feature_ref[...], (((0,), (0,)), ((), ())), preferred_element_type=F32
    )

    degree_ref[...] = jnp.zeros_like(degree_ref)

    def stage_copy(at):
        return pltpu.make_async_copy(stage.at[at], adjacency_ref.at[at], stage_sem.at[at])

    counted = jnp.zeros((8, 128), F32)
    for piece in range(per_block):
        for side in range(2):
            first = (2 * piece + side) * width
            columns = pl.ds(side * 128, 128)

            def unpack(step, sums, first=first, columns=columns, piece=piece):
                rows = pl.ds(pl.multiple_of(first + step * strip, 16), strip)
                packed = tables[0][rows, :]
                for table in tables[1:]:
                    packed = packed + table[rows, :]
                out = pl.ds(pl.multiple_of(step * strip, 16), strip)
                after = []
                for field in range(4):
                    value = packed if field == 0 else lax.shift_right_logical(packed, 8 * field)
                    value = (value if field == 3 else value & 255).astype(F32)
                    stage[field * per_block + piece, out, columns] = value.astype(BF16)
                    after.append(sums[field] + jnp.sum(value.reshape(strip // 8, 8, 128), axis=0))
                return tuple(after)

            sums = lax.fori_loop(0, width // strip, unpack, (jnp.zeros((8, 128), F32),) * 4)
            for field in range(4):
                degree_ref[field, pl.ds(piece, 1), columns] = jnp.sum(sums[field], axis=0, keepdims=True)
                counted = counted + sums[field]
        for field in range(4):
            stage_copy(field * per_block + piece).start()
    for at in range(blocks * per_block):
        stage_copy(at).wait()

    @pl.when(jnp.sum(counted).astype(jnp.int32) != tiles * 128)
    def _():
        table = tables[0]

        def field_pass(field, carry):
            clear(tables[:1])

            def one(edge, carry):
                word = word_ref[0, edge]
                match = jnp.where(lax.shift_right_logical(word, 7) % 4 == field, 1, 0)
                rows = pl.ds(lax.shift_right_logical(word, 9), 1)
                table[rows, :] = table[rows, :] + unit[pl.ds(word & 127, 1), :] * match
                return carry

            lax.fori_loop(0, tiles * 128, one, 0)
            for piece in range(per_block):
                for side in range(2):
                    value = table[pl.ds((2 * piece + side) * width, width), :].astype(F32)
                    columns = pl.ds(side * 128, 128)
                    stage[field * per_block + piece, :, columns] = value.astype(BF16)
                    degree_ref[field, pl.ds(piece, 1), columns] = jnp.sum(value, axis=0, keepdims=True)
            return carry

        lax.fori_loop(0, 4, field_pass, 0)
        for at in range(blocks * per_block):
            stage_copy(at).start()
        for at in range(blocks * per_block):
            stage_copy(at).wait()


def layer_kernel(doms, adjacency_ref, degree_ref, picked_ref, feature_hbm, cotangent_hbm, self_hbm, neigh_hbm,
                 bias_hbm, act_hbm, grad_hbm, returned_hbm,
                 feature_ref, cotangent_ref, self_ref, neigh_ref, bias_ref, act_ref, grad_ref,
                 adjacency, table_t, halo, halo_t, degree_in, inverse, own_pre,
                 foreign, kept, to_sibling, from_sibling, chip_out, chip_in, own_out, own_in, spread,
                 halo_grad, returned,
                 in_sem, out_sem, load_sem, halo_send, halo_recv, degree_send, degree_recv, part_send, part_recv, grad_send, grad_recv,
                 back_send, back_recv):
    part, source = lax.axis_index("dom"), lax.axis_index("src")
    chip, core = source // 2, source % 2
    sibling = chip * 2 + (1 - core)
    opposite = (1 - chip) * 2 + core
    diagonal = (1 - chip) * 2 + (1 - core)
    rows = feature_ref.shape[0]
    per_block = rows // CHUNK
    capacity = halo.shape[0] // doms

    barrier = pltpu.get_barrier_semaphore()
    for step in range(1, 4):
        pl.semaphore_signal(barrier, inc=1, device_id=(part, lax.rem(source + step, 4)), device_id_type=MESH)

    def greet(step, carry):
        pl.semaphore_signal(barrier, inc=1, device_id=(lax.rem(part + step, doms), source), device_id_type=MESH)
        return carry

    lax.fori_loop(1, doms, greet, 0)

    def load(chunk):
        return pltpu.make_async_copy(adjacency_ref.at[chunk], adjacency.at[chunk], load_sem.at[chunk])

    def load_block(block):
        def go(step, carry):
            load(block * per_block + step).start()
            return carry

        lax.fori_loop(0, per_block, go, 0)

    incoming = [
        pltpu.make_async_copy(whole, here, in_sem.at[at])
        for at, (whole, here) in enumerate((
            (feature_hbm, feature_ref), (self_hbm, self_ref), (neigh_hbm, neigh_ref), (bias_hbm, bias_ref),
            (cotangent_hbm, cotangent_ref), (degree_ref.at[source], degree_in.at[0]),
        ))
    ]
    incoming[0].start()
    load_block(diagonal)
    load_block(opposite)
    for copy in incoming[1:]:
        copy.start()
    load_block(sibling)
    load_block(source)
    incoming[0].wait()
    table_t[...] = feature_ref[...].astype(F32).T.astype(BF16)
    pl.semaphore_wait(barrier, 3 + doms - 1)

    def slot(at):
        return pl.ds(pl.multiple_of(at * capacity, capacity), capacity)

    def halo_copy(step):
        peer = lax.rem(part + step, doms)
        return pltpu.make_async_remote_copy(
            src_ref=picked_ref.at[slot(peer)], dst_ref=halo.at[slot(part)],
            send_sem=halo_send.at[step], recv_sem=halo_recv.at[step],
            device_id=(peer, source), device_id_type=MESH)

    def back_copy(step):
        peer = lax.rem(part + step, doms)
        return pltpu.make_async_remote_copy(
            src_ref=halo_grad.at[slot(peer)], dst_ref=returned.at[slot(part)],
            send_sem=back_send.at[step], recv_sem=back_recv.at[step],
            device_id=(peer, source), device_id_type=MESH)

    def each_peer(action):
        def go(step, carry):
            action(step)
            return carry

        lax.fori_loop(1, doms, go, 0)

    each_peer(lambda step: halo_copy(step).start())

    def degree_copy(step):
        peer = lax.rem(source + step, 4)
        return pltpu.make_async_remote_copy(
            src_ref=degree_ref.at[peer], dst_ref=degree_in.at[step],
            send_sem=degree_send.at[step], recv_sem=degree_recv.at[step],
            device_id=(part, peer), device_id_type=MESH)

    for step in range(1, 4):
        degree_copy(step).start()

    def part_copy(kind, step):
        source_ref, target_ref, peer = (
            (to_sibling, from_sibling, sibling),
            (chip_out, chip_in, opposite),
            (own_out, own_in, sibling),
        )[kind]
        return pltpu.make_async_remote_copy(
            src_ref=source_ref.at[step], dst_ref=target_ref.at[step],
            send_sem=part_send.at[kind, step], recv_sem=part_recv.at[kind, step],
            device_id=(part, peer), device_id_type=MESH)

    def grad_copy(kind, step):
        owner, peer = ((source, sibling), (source, opposite), (opposite, sibling))[kind]
        at = owner * per_block + step
        return pltpu.make_async_remote_copy(
            src_ref=spread.at[at], dst_ref=spread.at[at],
            send_sem=grad_send.at[kind, step], recv_sem=grad_recv.at[kind, step],
            device_id=(part, peer), device_id_type=MESH)

    def each_chunk(action):
        def go(step, carry):
            action(step)
            return carry

        lax.fori_loop(0, per_block, go, 0)

    def from_local(at):
        return jnp.dot(table_t[...], adjacency[at, 0:rows, :], preferred_element_type=F32)

    def from_halo(at):
        return jnp.dot(halo_t[...], adjacency[at, rows:, :], preferred_element_type=F32)

    def early(step):
        at = diagonal * per_block + step
        load(at).wait()
        foreign[step] = from_local(at)

    def early_kept(step):
        at = opposite * per_block + step
        load(at).wait()
        kept[step] = from_local(at)

    each_chunk(early)
    each_chunk(early_kept)
    halo[slot(part), :] = jnp.zeros((capacity, halo.shape[1]), F32)
    returned[slot(part), :] = jnp.zeros((capacity, halo.shape[1]), F32)
    each_peer(lambda step: halo_copy(step).wait_recv())
    halo_t[...] = halo[...].T.astype(BF16)

    def send_foreign(step):
        to_sibling[step] = (foreign[step] + from_halo(diagonal * per_block + step)).astype(BF16)
        part_copy(0, step).start()

    each_chunk(send_foreign)

    def send_chip(step):
        mine = kept[step] + from_halo(opposite * per_block + step)
        part_copy(0, step).wait_recv()
        chip_out[step] = (mine + from_sibling[step].astype(F32)).astype(BF16)
        part_copy(1, step).start()

    send_chip(0)
    send_chip(1)

    def send_own(step):
        at = sibling * per_block + step
        load(at).wait()
        own_out[step] = (from_local(at) + from_halo(at)).astype(BF16)
        part_copy(2, step).start()

    each_chunk(send_own)

    def keep_own(step):
        at = source * per_block + step
        load(at).wait()
        foreign[step] = from_local(at) + from_halo(at)

    each_chunk(keep_own)
    for copy in incoming[1:]:
        copy.wait()
    own_pre[...] = jnp.dot(feature_ref[...], self_ref[...], preferred_element_type=F32) + bias_ref[...].astype(F32).reshape(1, -1)

    degree = degree_in[0]
    for step in range(1, 4):
        degree_copy(step).wait_recv()
        degree = degree + degree_in[step]
    inverse[...] = 1.0 / jnp.maximum(degree, 1.0)
    halo_grad[...] = jnp.zeros_like(halo_grad)
    grad_ref[...] = jnp.zeros_like(grad_ref)

    def back_halo(at):
        halo_grad[...] += jnp.dot(adjacency[at, rows:, :], spread[at], preferred_element_type=F32)

    def back_local(at):
        grad_ref[...] += jnp.dot(adjacency[at, 0:rows, :], spread[at], preferred_element_type=F32)

    def back_own(step):
        at = source * per_block + step
        back_halo(at)
        back_local(at)

    def back_sibling(step):
        at = sibling * per_block + step
        grad_copy(0, step).wait_recv()
        back_halo(at)
        back_local(at)

    def act_copy(step):
        here = pl.ds(pl.multiple_of(step * CHUNK, CHUNK), CHUNK)
        return pltpu.make_async_copy(act_ref.at[here], act_hbm.at[here], out_sem.at[step])

    def dense(step):
        here = pl.ds(pl.multiple_of(step * CHUNK, CHUNK), CHUNK)
        inverse_row = inverse[pl.ds(step, 1), :]
        half = jnp.broadcast_to(inverse_row, (128, CHUNK)).T
        inverse_column = jnp.concatenate([half] * (act_ref.shape[1] // 128), axis=1)
        part_copy(2, step).wait_recv()
        part_copy(1, step).wait_recv()
        total_t = foreign[step] + own_in[step].astype(F32) + chip_in[step].astype(F32)
        mean = (total_t * inverse_row).T.astype(BF16)
        preact = own_pre[here, :] + jnp.dot(mean, neigh_ref[...], preferred_element_type=F32)
        sigma = jax.nn.sigmoid(preact)
        slope = sigma * (1.0 + preact * (1.0 - sigma))
        upstream = (cotangent_ref[here, :].astype(F32) * slope).astype(BF16)
        contract = (((1,), (1,)), ((), ()))
        at = source * per_block + step
        spread[at] = (
            lax.dot_general(upstream, neigh_ref[...], contract, preferred_element_type=F32) * inverse_column
        ).astype(BF16)
        grad_copy(1, step).start()
        grad_copy(0, step).start()
        act_ref[here, :] = (preact * sigma).astype(BF16)
        act_copy(step).start()
        grad_ref[here, :] += lax.dot_general(upstream, self_ref[...], contract, preferred_element_type=F32)

    for step in range(2, per_block):
        part_copy(1, step - 2).wait_send()
        send_chip(step)
        dense(step - 2)
        back_own(step - 2)
    for step in range(per_block - 2, per_block):
        grad_copy(1, step - 2).wait_send()
        dense(step)
        back_own(step)
    for step in range(per_block):
        back_sibling(step)
    last = per_block - 1
    for step in range(per_block):
        grad_copy(1, step).wait_recv()
        grad_copy(2, step).start()
        back_halo(opposite * per_block + step)
        if step < last:
            back_local(opposite * per_block + step)
        if step > 0:
            grad_copy(2, step - 1).wait_recv()
            back_halo(diagonal * per_block + step - 1)
            back_local(diagonal * per_block + step - 1)
    grad_copy(2, last).wait_recv()
    back_halo(diagonal * per_block + last)
    each_peer(lambda step: back_copy(step).start())
    back_local(opposite * per_block + last)
    back_local(diagonal * per_block + last)

    grad_out = pltpu.make_async_copy(grad_ref, grad_hbm, out_sem.at[per_block])
    grad_out.start()
    each_peer(lambda step: back_copy(step).wait_recv())
    returned_out = pltpu.make_async_copy(returned, returned_hbm, out_sem.at[per_block + 1])
    returned_out.start()
    each_peer(lambda step: halo_copy(step).wait_send())
    each_peer(lambda step: back_copy(step).wait_send())
    for step in range(1, 4):
        degree_copy(step).wait_send()
    each_chunk(lambda step: act_copy(step).wait())
    for kind in range(3):
        for step in range(per_block - 2 if kind == 1 else 0, per_block):
            part_copy(kind, step).wait_send()
            grad_copy(kind, step).wait_send()
    grad_out.wait()
    returned_out.wait()


def finish_kernel(part_act_ref, part_grad_ref, returned_ref, row_ref, act_ref, grad_ref, grad, returned, sem):
    pieces = grad_ref.shape[0] // CHUNK

    def piece(at):
        return pl.ds(at * CHUNK, CHUNK)

    act = pltpu.make_async_copy(part_act_ref, act_ref, sem.at[0])
    back = pltpu.make_async_copy(returned_ref, returned, sem.at[1])
    come = [
        pltpu.make_async_copy(part_grad_ref.at[piece(at)], grad.at[piece(at)], sem.at[2 + at]) for at in range(pieces)
    ]
    back.start()
    for copy in come:
        copy.start()
    act.start()
    back.wait()
    rows = returned[...].astype(BF16)
    leave = []
    for at in range(pieces):
        chosen = lax.broadcasted_iota(jnp.int32, (CHUNK, row_ref.shape[1]), 0) + at * CHUNK == row_ref[...]
        added = jnp.dot(chosen.astype(F32).astype(BF16), rows, preferred_element_type=F32)
        come[at].wait()
        grad[piece(at), :] += added
        leave.append(pltpu.make_async_copy(grad.at[piece(at)], grad_ref.at[piece(at)], sem.at[2 + pieces + at]))
        leave[-1].start()
    act.wait()
    for copy in leave:
        copy.wait()


def local(features, cotangent, w_self, w_neigh, bias, send_rows, edge_src, edge_dst, tile_count):
    rows, features_wide = features.shape
    doms, columns = lax.axis_size("dom"), lax.axis_size("src")
    slots = send_rows.shape[2] * send_rows.shape[3]
    width = rows + slots
    chunks = rows * columns // CHUNK
    per_block = rows // CHUNK
    edges = edge_src.shape[2]
    limit = (36 if width <= 1152 else 58) * 1024 * 1024
    vmem = pl.BlockSpec(memory_space=pltpu.VMEM)
    smem = pl.BlockSpec(memory_space=pltpu.SMEM)
    anywhere = pl.BlockSpec(memory_space=pl.ANY)

    adjacency, degree, picked, row = pl.pallas_call(
        functools.partial(build_kernel, width),
        out_shape=(
            jax.ShapeDtypeStruct((chunks, width, CHUNK), BF16),
            jax.ShapeDtypeStruct((columns, 8, CHUNK), F32),
            jax.ShapeDtypeStruct((slots, features_wide), F32),
            jax.ShapeDtypeStruct((1, slots), jnp.int32),
        ),
        in_specs=[anywhere, anywhere, anywhere, smem, vmem],
        out_specs=(anywhere, vmem, vmem, vmem),
        scratch_shapes=[
            pltpu.VMEM((1, edges), jnp.int32),
            pltpu.VMEM((1, edges), jnp.int32),
            pltpu.VMEM((rows, features_wide), BF16),
            pltpu.VMEM((1, edges), jnp.int32),
            pltpu.SMEM((1, edges), jnp.int32),
            pltpu.VMEM((520, 128), jnp.int32),
            pltpu.VMEM((chunks, width, CHUNK), BF16),
            pltpu.SemaphoreType.DMA((4,)),
            pltpu.SemaphoreType.DMA((chunks,)),
        ] + [pltpu.VMEM((rows // 128 * width, 128), jnp.int32)] * 4,
        compiler_params=pltpu.CompilerParams(vmem_limit_bytes=limit),
        name="count_edges",
    )(edge_src, edge_dst, features, tile_count.reshape(1), send_rows)

    wide = features_wide
    dma = pltpu.SemaphoreType.DMA
    block_half = pltpu.VMEM((per_block, wide, CHUNK), BF16)
    block_full = pltpu.VMEM((per_block, wide, CHUNK), F32)
    part_act, part_grad, returned = pl.pallas_call(
        functools.partial(layer_kernel, doms),
        out_shape=(
            jax.ShapeDtypeStruct((rows, wide), BF16),
            jax.ShapeDtypeStruct((rows, wide), F32),
            jax.ShapeDtypeStruct((slots, wide), F32),
        ),
        in_specs=[anywhere] * 8,
        out_specs=(anywhere, anywhere, anywhere),
        scratch_shapes=[
            pltpu.VMEM((rows, wide), BF16),
            pltpu.VMEM((rows, wide), BF16),
            pltpu.VMEM(w_self.shape, BF16),
            pltpu.VMEM(w_neigh.shape, BF16),
            pltpu.VMEM(bias.shape, BF16),
            pltpu.VMEM((rows, wide), BF16),
            pltpu.VMEM((rows, wide), F32),
            pltpu.VMEM((chunks, width, CHUNK), BF16),
            pltpu.VMEM((wide, rows), BF16),
            pltpu.VMEM((slots, wide), F32),
            pltpu.VMEM((wide, slots), BF16),
            pltpu.VMEM((4, 8, CHUNK), F32),
            pltpu.VMEM((8, CHUNK), F32),
            pltpu.VMEM((rows, wide), F32),
            block_full, block_full,
            block_half, block_half, block_half, block_half, block_half, block_half,
            pltpu.VMEM((chunks, CHUNK, wide), BF16),
            pltpu.VMEM((slots, wide), F32),
            pltpu.VMEM((slots, wide), F32),
            dma((6,)), dma((per_block + 2,)), dma((chunks,)),
            dma((doms,)), dma((doms,)),
            dma((4,)), dma((4,)),
            dma((3, per_block)), dma((3, per_block)),
            dma((3, per_block)), dma((3, per_block)),
            dma((doms,)), dma((doms,)),
        ],
        compiler_params=pltpu.CompilerParams(
            collective_id=0, has_side_effects=True, vmem_limit_bytes=limit
        ),
        name="layer",
    )(adjacency, degree, picked, features, cotangent, w_self, w_neigh, bias)

    return pl.pallas_call(
        finish_kernel,
        out_shape=(
            jax.ShapeDtypeStruct((rows, wide), BF16),
            jax.ShapeDtypeStruct((rows, wide), F32),
        ),
        in_specs=[anywhere, anywhere, anywhere, vmem],
        out_specs=(anywhere, anywhere),
        scratch_shapes=[pltpu.VMEM((rows, wide), F32), pltpu.VMEM((slots, wide), F32), dma((2 + 2 * per_block,))],
        compiler_params=pltpu.CompilerParams(vmem_limit_bytes=limit),
        name="finish",
    )(part_act, part_grad, returned, row)


def solution(mesh):
    placed = (
        P(("dom", "src"), None),
        P(("dom", "src"), None),
        P(),
        P(),
        P(),
        P("dom", "src", None, None),
        P("dom", "src", None),
        P("dom", "src", None),
        P("dom", "src"),
    )
    return jax.shard_map(
        local,
        mesh=mesh,
        in_specs=placed,
        out_specs=(P(("dom", "src"), None), P(("dom", "src"), None)),
        check_vma=False,
    )
```

```python
import functools

import jax
import jax.numpy as jnp
from jax import lax
from jax.experimental import pallas as pl
from jax.experimental.pallas import tpu as pltpu
from jax.sharding import PartitionSpec as P

MESH = pl.DeviceIdType.MESH
CHUNK = 256
STRIP = 64
F32 = jnp.float32
BF16 = jnp.bfloat16


def strip_of(width):
    return max(rows for rows in range(16, 321, 16) if width % rows == 0)


def build_kernel(width, source_hbm, target_hbm, feature_hbm, sender_hbm, count_ref,
                 adjacency_ref, degree_ref, picked_ref, row_ref,
                 source_ref, target_ref, feature_ref, sender_ref, word_vmem, word_ref, keys, even, odd, stage,
                 in_sem, stage_sem, *tables):
    incoming = [
        pltpu.make_async_copy(source_hbm.at[0], source_ref, in_sem.at[0]),
        pltpu.make_async_copy(target_hbm.at[0], target_ref, in_sem.at[1]),
        pltpu.make_async_copy(feature_hbm, feature_ref, in_sem.at[2]),
        pltpu.make_async_copy(sender_hbm, sender_ref, in_sem.at[4]),
    ]
    for copy in incoming:
        copy.start()
    total_rows = tables[0].shape[0]
    lanes = len(tables)
    accounts = feature_ref.shape[0]
    per_block = accounts // CHUNK
    blocks = stage.shape[0] // per_block
    strip = strip_of(width)
    tiles = count_ref[0]

    incoming[0].wait()
    incoming[1].wait()
    edges = target_ref.shape[1]
    target = target_ref[...]
    within = target % accounts
    word_vmem[...] = (within // 128) * width + source_ref[...]
    word_copy = pltpu.make_async_copy(word_vmem, word_ref, in_sem.at[3])
    word_copy.start()
    key = (target // accounts) * 128 + within % 128
    for tile in range(edges // 128):
        keys[tile : tile + 1, :] = key[:, tile * 128 : tile * 128 + 128]

    zeros = jnp.zeros((128, 128), jnp.int32)

    def clear(chosen):
        def go(step, carry):
            for table in chosen:
                table[pl.ds(pl.multiple_of(step * 128, 128), 128), :] = zeros
            return carry

        lax.fori_loop(0, total_rows // 128, go, 0)

    clear(tables)
    word_copy.wait()
    incoming[2].wait()
    incoming[3].wait()

    lane_at = lax.broadcasted_iota(jnp.int32, (128, 128), 1)

    def one_hot(out, tile):
        held = jnp.minimum(tile, edges // 128 - 1)
        key = jnp.broadcast_to(keys[pl.ds(held, 1), :], (128, 128)).T
        amount = lax.shift_left(jnp.where(tile < tiles, 1, 0), lax.shift_right_logical(key, 7) * 8)
        out[...] = jnp.where(lane_at == (key & 127), amount, 0)

    def add_tile(rows_of, tile):
        base = jnp.minimum(tile, edges // 128 - 1) * 128
        for group in range(0, 128, lanes):
            rows = [pl.ds(word_ref[0, base + group + k], 1) for k in range(lanes)]
            sums = [tables[k][rows[k], :] + rows_of[group + k : group + k + 1, :] for k in range(lanes)]
            for k in range(lanes):
                tables[k][rows[k], :] = sums[k]

    def edge_tiles(pair, carry):
        one_hot(odd, 2 * pair + 1)
        add_tile(even, 2 * pair)
        one_hot(even, 2 * pair + 2)
        add_tile(odd, 2 * pair + 1)
        return carry

    one_hot(even, 0)
    lax.fori_loop(0, (tiles + 1) // 2, edge_tiles, 0)

    peers, capacity = sender_ref.shape[2:]
    slots = peers * capacity
    sender = sender_ref[0, 0]
    repeat = (
        lax.broadcasted_iota(jnp.int32, (capacity, slots), 1) % capacity
        == lax.broadcasted_iota(jnp.int32, (capacity, slots), 0)
    ).astype(F32).astype(BF16)
    high = jnp.dot(lax.shift_right_arithmetic(sender, 5).astype(F32).astype(BF16), repeat, preferred_element_type=F32)
    low = jnp.dot((sender & 31).astype(F32).astype(BF16), repeat, preferred_element_type=F32)
    mine = (
        lax.broadcasted_iota(jnp.int32, (peers, slots), 1) // capacity
        == lax.broadcasted_iota(jnp.int32, (peers, slots), 0)
    )
    row = jnp.sum(jnp.where(mine, high * 32.0 + low, 0.0), axis=0, keepdims=True).astype(jnp.int32)
    row_ref[...] = row
    chosen = lax.broadcasted_iota(jnp.int32, (accounts, slots), 0) == row
    picked_ref[...] = lax.dot_general(
        chosen.astype(F32).astype(BF16), feature_ref[...], (((0,), (0,)), ((), ())), preferred_element_type=F32
    )

    degree_ref[...] = jnp.zeros_like(degree_ref)

    def stage_copy(at):
        return pltpu.make_async_copy(stage.at[at], adjacency_ref.at[at], stage_sem.at[at])

    counted = jnp.zeros((8, 128), F32)
    for piece in range(per_block):
        for side in range(2):
            first = (2 * piece + side) * width
            columns = pl.ds(side * 128, 128)

            def unpack(step, sums, first=first, columns=columns, piece=piece):
                rows = pl.ds(pl.multiple_of(first + step * strip, 16), strip)
                packed = tables[0][rows, :]
                for table in tables[1:]:
                    packed = packed + table[rows, :]
                out = pl.ds(pl.multiple_of(step * strip, 16), strip)
                after = []
                for field in range(4):
                    value = packed if field == 0 else lax.shift_right_logical(packed, 8 * field)
                    value = (value if field == 3 else value & 255).astype(F32)
                    stage[field * per_block + piece, out, columns] = value.astype(BF16)
                    after.append(sums[field] + jnp.sum(value.reshape(strip // 8, 8, 128), axis=0))
                return tuple(after)

            sums = lax.fori_loop(0, width // strip, unpack, (jnp.zeros((8, 128), F32),) * 4)
            for field in range(4):
                degree_ref[field, pl.ds(piece, 1), columns] = jnp.sum(sums[field], axis=0, keepdims=True)
                counted = counted + sums[field]
        for field in range(4):
            stage_copy(field * per_block + piece).start()
    for at in range(blocks * per_block):
        stage_copy(at).wait()

    @pl.when(jnp.sum(counted).astype(jnp.int32) != tiles * 128)
    def _():
        table = tables[0]

        def field_pass(field, carry):
            clear(tables[:1])

            def one(edge, carry):
                rows = pl.ds(word_ref[0, edge], 1)
                amount = even[pl.ds(edge % 128, 1), :]
                match = lax.shift_right_logical(amount, 8 * field) & 255
                table[rows, :] = table[rows, :] + match
                return carry

            def tile_pass(tile, carry):
                one_hot(even, tile)
                return lax.fori_loop(tile * 128, tile * 128 + 128, one, carry)

            lax.fori_loop(0, tiles, tile_pass, 0)
            for piece in range(per_block):
                for side in range(2):
                    value = table[pl.ds((2 * piece + side) * width, width), :].astype(F32)
                    columns = pl.ds(side * 128, 128)
                    stage[field * per_block + piece, :, columns] = value.astype(BF16)
                    degree_ref[field, pl.ds(piece, 1), columns] = jnp.sum(value, axis=0, keepdims=True)
            return carry

        lax.fori_loop(0, 4, field_pass, 0)
        for at in range(blocks * per_block):
            stage_copy(at).start()
        for at in range(blocks * per_block):
            stage_copy(at).wait()


def layer_kernel(doms, adjacency_ref, degree_ref, picked_ref, feature_hbm, cotangent_hbm, self_hbm, neigh_hbm,
                 bias_hbm, act_hbm, grad_hbm, returned_hbm,
                 feature_ref, cotangent_ref, self_ref, neigh_ref, bias_ref, act_ref, grad_ref,
                 adjacency, table_t, halo, halo_t, degree_in, inverse, own_pre,
                 foreign, kept, to_sibling, from_sibling, chip_out, chip_in, own_out, own_in, spread,
                 halo_grad, returned,
                 in_sem, out_sem, load_sem, halo_send, halo_recv, degree_send, degree_recv, part_send, part_recv, grad_send, grad_recv,
                 back_send, back_recv):
    part, source = lax.axis_index("dom"), lax.axis_index("src")
    chip, core = source // 2, source % 2
    sibling = chip * 2 + (1 - core)
    opposite = (1 - chip) * 2 + core
    diagonal = (1 - chip) * 2 + (1 - core)
    rows = feature_ref.shape[0]
    per_block = rows // CHUNK
    capacity = halo.shape[0] // doms

    barrier = pltpu.get_barrier_semaphore()
    for step in range(1, 4):
        pl.semaphore_signal(barrier, inc=1, device_id=(part, lax.rem(source + step, 4)), device_id_type=MESH)

    def greet(step, carry):
        pl.semaphore_signal(barrier, inc=1, device_id=(lax.rem(part + step, doms), source), device_id_type=MESH)
        return carry

    lax.fori_loop(1, doms, greet, 0)

    def load(chunk):
        return pltpu.make_async_copy(adjacency_ref.at[chunk], adjacency.at[chunk], load_sem.at[chunk])

    def load_block(block):
        def go(step, carry):
            load(block * per_block + step).start()
            return carry

        lax.fori_loop(0, per_block, go, 0)

    incoming = [
        pltpu.make_async_copy(whole, here, in_sem.at[at])
        for at, (whole, here) in enumerate((
            (feature_hbm, feature_ref), (self_hbm, self_ref), (neigh_hbm, neigh_ref), (bias_hbm, bias_ref),
            (cotangent_hbm, cotangent_ref), (degree_ref.at[source], degree_in.at[0]),
        ))
    ]
    incoming[0].start()
    load_block(diagonal)
    load_block(opposite)
    for copy in incoming[1:]:
        copy.start()
    load_block(sibling)
    load_block(source)
    incoming[0].wait()
    table_t[...] = feature_ref[...].astype(F32).T.astype(BF16)
    pl.semaphore_wait(barrier, 3 + doms - 1)

    def slot(at):
        return pl.ds(pl.multiple_of(at * capacity, capacity), capacity)

    def halo_copy(step):
        peer = lax.rem(part + step, doms)
        return pltpu.make_async_remote_copy(
            src_ref=picked_ref.at[slot(peer)], dst_ref=halo.at[slot(part)],
            send_sem=halo_send.at[step], recv_sem=halo_recv.at[step],
            device_id=(peer, source), device_id_type=MESH)

    def back_copy(step):
        peer = lax.rem(part + step, doms)
        return pltpu.make_async_remote_copy(
            src_ref=halo_grad.at[slot(peer)], dst_ref=returned.at[slot(part)],
            send_sem=back_send.at[step], recv_sem=back_recv.at[step],
            device_id=(peer, source), device_id_type=MESH)

    def each_peer(action):
        def go(step, carry):
            action(step)
            return carry

        lax.fori_loop(1, doms, go, 0)

    each_peer(lambda step: halo_copy(step).start())

    def degree_copy(step):
        peer = lax.rem(source + step, 4)
        return pltpu.make_async_remote_copy(
            src_ref=degree_ref.at[peer], dst_ref=degree_in.at[step],
            send_sem=degree_send.at[step], recv_sem=degree_recv.at[step],
            device_id=(part, peer), device_id_type=MESH)

    for step in range(1, 4):
        degree_copy(step).start()

    def part_copy(kind, step):
        source_ref, target_ref, peer = (
            (to_sibling, from_sibling, sibling),
            (chip_out, chip_in, opposite),
            (own_out, own_in, sibling),
        )[kind]
        return pltpu.make_async_remote_copy(
            src_ref=source_ref.at[step], dst_ref=target_ref.at[step],
            send_sem=part_send.at[kind, step], recv_sem=part_recv.at[kind, step],
            device_id=(part, peer), device_id_type=MESH)

    def grad_copy(kind, step):
        owner, peer = ((source, sibling), (source, opposite), (opposite, sibling))[kind]
        at = owner * per_block + step
        return pltpu.make_async_remote_copy(
            src_ref=spread.at[at], dst_ref=spread.at[at],
            send_sem=grad_send.at[kind, step], recv_sem=grad_recv.at[kind, step],
            device_id=(part, peer), device_id_type=MESH)

    def each_chunk(action):
        def go(step, carry):
            action(step)
            return carry

        lax.fori_loop(0, per_block, go, 0)

    def from_local(at):
        return jnp.dot(table_t[...], adjacency[at, 0:rows, :], preferred_element_type=F32)

    def from_halo(at):
        return jnp.dot(halo_t[...], adjacency[at, rows:, :], preferred_element_type=F32)

    def early(step):
        at = diagonal * per_block + step
        load(at).wait()
        foreign[step] = from_local(at)

    def early_kept(step):
        at = opposite * per_block + step
        load(at).wait()
        kept[step] = from_local(at)

    each_chunk(early)
    each_chunk(early_kept)
    halo[slot(part), :] = jnp.zeros((capacity, halo.shape[1]), F32)
    returned[slot(part), :] = jnp.zeros((capacity, halo.shape[1]), F32)
    each_peer(lambda step: halo_copy(step).wait_recv())
    halo_t[...] = halo[...].T.astype(BF16)

    def send_foreign(step):
        to_sibling[step] = (foreign[step] + from_halo(diagonal * per_block + step)).astype(BF16)
        part_copy(0, step).start()

    each_chunk(send_foreign)

    def send_chip(step):
        mine = kept[step] + from_halo(opposite * per_block + step)
        part_copy(0, step).wait_recv()
        chip_out[step] = (mine + from_sibling[step].astype(F32)).astype(BF16)
        part_copy(1, step).start()

    send_chip(0)
    send_chip(1)

    def send_own(step):
        at = sibling * per_block + step
        load(at).wait()
        own_out[step] = (from_local(at) + from_halo(at)).astype(BF16)
        part_copy(2, step).start()

    each_chunk(send_own)

    def keep_own(step):
        at = source * per_block + step
        load(at).wait()
        foreign[step] = from_local(at) + from_halo(at)

    each_chunk(keep_own)
    for copy in incoming[1:]:
        copy.wait()
    own_pre[...] = jnp.dot(feature_ref[...], self_ref[...], preferred_element_type=F32) + bias_ref[...].astype(F32).reshape(1, -1)

    degree = degree_in[0]
    for step in range(1, 4):
        degree_copy(step).wait_recv()
        degree = degree + degree_in[step]
    inverse[...] = 1.0 / jnp.maximum(degree, 1.0)
    halo_grad[...] = jnp.zeros_like(halo_grad)
    grad_ref[...] = jnp.zeros_like(grad_ref)

    def back_halo(at):
        halo_grad[...] += jnp.dot(adjacency[at, rows:, :], spread[at], preferred_element_type=F32)

    def back_local(at):
        grad_ref[...] += jnp.dot(adjacency[at, 0:rows, :], spread[at], preferred_element_type=F32)

    def back_own(step):
        at = source * per_block + step
        back_halo(at)
        back_local(at)

    def back_sibling(step):
        at = sibling * per_block + step
        grad_copy(0, step).wait_recv()
        back_halo(at)
        back_local(at)

    def act_copy(step):
        here = pl.ds(pl.multiple_of(step * CHUNK, CHUNK), CHUNK)
        return pltpu.make_async_copy(act_ref.at[here], act_hbm.at[here], out_sem.at[step])

    def dense(step):
        here = pl.ds(pl.multiple_of(step * CHUNK, CHUNK), CHUNK)
        inverse_row = inverse[pl.ds(step, 1), :]
        half = jnp.broadcast_to(inverse_row, (128, CHUNK)).T
        inverse_column = jnp.concatenate([half] * (act_ref.shape[1] // 128), axis=1)
        part_copy(2, step).wait_recv()
        part_copy(1, step).wait_recv()
        total_t = foreign[step] + own_in[step].astype(F32) + chip_in[step].astype(F32)
        mean = (total_t * inverse_row).T.astype(BF16)
        preact = own_pre[here, :] + jnp.dot(mean, neigh_ref[...], preferred_element_type=F32)
        sigma = jax.nn.sigmoid(preact)
        slope = sigma * (1.0 + preact * (1.0 - sigma))
        upstream = (cotangent_ref[here, :].astype(F32) * slope).astype(BF16)
        contract = (((1,), (1,)), ((), ()))
        at = source * per_block + step
        spread[at] = (
            lax.dot_general(upstream, neigh_ref[...], contract, preferred_element_type=F32) * inverse_column
        ).astype(BF16)
        grad_copy(1, step).start()
        grad_copy(0, step).start()
        act_ref[here, :] = (preact * sigma).astype(BF16)
        act_copy(step).start()
        grad_ref[here, :] += lax.dot_general(upstream, self_ref[...], contract, preferred_element_type=F32)

    for step in range(2, per_block):
        part_copy(1, step - 2).wait_send()
        send_chip(step)
        dense(step - 2)
        back_own(step - 2)
    for step in range(per_block - 2, per_block):
        grad_copy(1, step - 2).wait_send()
        dense(step)
        back_own(step)
    for step in range(per_block):
        back_sibling(step)
    last = per_block - 1
    for step in range(per_block):
        grad_copy(1, step).wait_recv()
        grad_copy(2, step).start()
        back_halo(opposite * per_block + step)
        if step < last:
            back_local(opposite * per_block + step)
        if step > 0:
            grad_copy(2, step - 1).wait_recv()
            back_halo(diagonal * per_block + step - 1)
            back_local(diagonal * per_block + step - 1)
    grad_copy(2, last).wait_recv()
    back_halo(diagonal * per_block + last)
    each_peer(lambda step: back_copy(step).start())
    back_local(opposite * per_block + last)
    back_local(diagonal * per_block + last)

    grad_out = pltpu.make_async_copy(grad_ref, grad_hbm, out_sem.at[per_block])
    grad_out.start()
    each_peer(lambda step: back_copy(step).wait_recv())
    returned_out = pltpu.make_async_copy(returned, returned_hbm, out_sem.at[per_block + 1])
    returned_out.start()
    each_peer(lambda step: halo_copy(step).wait_send())
    each_peer(lambda step: back_copy(step).wait_send())
    for step in range(1, 4):
        degree_copy(step).wait_send()
    each_chunk(lambda step: act_copy(step).wait())
    for kind in range(3):
        for step in range(per_block - 2 if kind == 1 else 0, per_block):
            part_copy(kind, step).wait_send()
            grad_copy(kind, step).wait_send()
    grad_out.wait()
    returned_out.wait()


def finish_kernel(part_act_ref, part_grad_ref, returned_ref, row_ref, act_ref, grad_ref, grad, returned, sem):
    pieces = grad_ref.shape[0] // CHUNK

    def piece(at):
        return pl.ds(at * CHUNK, CHUNK)

    act = pltpu.make_async_copy(part_act_ref, act_ref, sem.at[0])
    back = pltpu.make_async_copy(returned_ref, returned, sem.at[1])
    come = [
        pltpu.make_async_copy(part_grad_ref.at[piece(at)], grad.at[piece(at)], sem.at[2 + at]) for at in range(pieces)
    ]
    back.start()
    for copy in come:
        copy.start()
    act.start()
    back.wait()
    rows = returned[...].astype(BF16)
    leave = []
    for at in range(pieces):
        chosen = lax.broadcasted_iota(jnp.int32, (CHUNK, row_ref.shape[1]), 0) + at * CHUNK == row_ref[...]
        added = jnp.dot(chosen.astype(F32).astype(BF16), rows, preferred_element_type=F32)
        come[at].wait()
        grad[piece(at), :] += added
        leave.append(pltpu.make_async_copy(grad.at[piece(at)], grad_ref.at[piece(at)], sem.at[2 + pieces + at]))
        leave[-1].start()
    act.wait()
    for copy in leave:
        copy.wait()


def local(features, cotangent, w_self, w_neigh, bias, send_rows, edge_src, edge_dst, tile_count):
    rows, features_wide = features.shape
    doms, columns = lax.axis_size("dom"), lax.axis_size("src")
    slots = send_rows.shape[2] * send_rows.shape[3]
    width = rows + slots
    chunks = rows * columns // CHUNK
    per_block = rows // CHUNK
    edges = edge_src.shape[2]
    limit = 58 * 1024 * 1024
    vmem = pl.BlockSpec(memory_space=pltpu.VMEM)
    smem = pl.BlockSpec(memory_space=pltpu.SMEM)
    anywhere = pl.BlockSpec(memory_space=pl.ANY)
    hbm = pl.BlockSpec(memory_space=pltpu.HBM)

    adjacency, degree, picked, row = pl.pallas_call(
        functools.partial(build_kernel, width),
        out_shape=(
            jax.ShapeDtypeStruct((chunks, width, CHUNK), BF16),
            jax.ShapeDtypeStruct((columns, 8, CHUNK), F32),
            jax.ShapeDtypeStruct((slots, features_wide), F32),
            jax.ShapeDtypeStruct((1, slots), jnp.int32),
        ),
        in_specs=[hbm, hbm, hbm, hbm, smem],
        out_specs=(anywhere, vmem, vmem, vmem),
        scratch_shapes=[
            pltpu.VMEM((1, edges), jnp.int32),
            pltpu.VMEM((1, edges), jnp.int32),
            pltpu.VMEM((rows, features_wide), BF16),
            pltpu.VMEM(send_rows.shape, jnp.int32),
            pltpu.VMEM((1, edges), jnp.int32),
            pltpu.SMEM((1, edges), jnp.int32),
            pltpu.VMEM((edges // 128, 128), jnp.int32),
            pltpu.VMEM((128, 128), jnp.int32),
            pltpu.VMEM((128, 128), jnp.int32),
            pltpu.VMEM((chunks, width, CHUNK), BF16),
            pltpu.SemaphoreType.DMA((5,)),
            pltpu.SemaphoreType.DMA((chunks,)),
        ] + [pltpu.VMEM((rows // 128 * width, 128), jnp.int32)] * 4,
        compiler_params=pltpu.CompilerParams(vmem_limit_bytes=limit),
        name="count_edges",
    )(edge_src, edge_dst, features, send_rows, tile_count.reshape(1))

    wide = features_wide
    dma = pltpu.SemaphoreType.DMA
    block_half = pltpu.VMEM((per_block, wide, CHUNK), BF16)
    block_full = pltpu.VMEM((per_block, wide, CHUNK), F32)
    part_act, part_grad, returned = pl.pallas_call(
        functools.partial(layer_kernel, doms),
        out_shape=(
            jax.ShapeDtypeStruct((rows, wide), BF16),
            jax.ShapeDtypeStruct((rows, wide), F32),
            jax.ShapeDtypeStruct((slots, wide), F32),
        ),
        in_specs=[anywhere] * 3 + [hbm] * 5,
        out_specs=(anywhere, anywhere, anywhere),
        scratch_shapes=[
            pltpu.VMEM((rows, wide), BF16),
            pltpu.VMEM((rows, wide), BF16),
            pltpu.VMEM(w_self.shape, BF16),
            pltpu.VMEM(w_neigh.shape, BF16),
            pltpu.VMEM(bias.shape, BF16),
            pltpu.VMEM((rows, wide), BF16),
            pltpu.VMEM((rows, wide), F32),
            pltpu.VMEM((chunks, width, CHUNK), BF16),
            pltpu.VMEM((wide, rows), BF16),
            pltpu.VMEM((slots, wide), F32),
            pltpu.VMEM((wide, slots), BF16),
            pltpu.VMEM((4, 8, CHUNK), F32),
            pltpu.VMEM((8, CHUNK), F32),
            pltpu.VMEM((rows, wide), F32),
            block_full, block_full,
            block_half, block_half, block_half, block_half, block_half, block_half,
            pltpu.VMEM((chunks, CHUNK, wide), BF16),
            pltpu.VMEM((slots, wide), F32),
            pltpu.VMEM((slots, wide), F32),
            dma((6,)), dma((per_block + 2,)), dma((chunks,)),
            dma((doms,)), dma((doms,)),
            dma((4,)), dma((4,)),
            dma((3, per_block)), dma((3, per_block)),
            dma((3, per_block)), dma((3, per_block)),
            dma((doms,)), dma((doms,)),
        ],
        compiler_params=pltpu.CompilerParams(
            collective_id=0, has_side_effects=True, vmem_limit_bytes=limit
        ),
        name="layer",
    )(adjacency, degree, picked, features, cotangent, w_self, w_neigh, bias)

    return pl.pallas_call(
        finish_kernel,
        out_shape=(
            jax.ShapeDtypeStruct((rows, wide), BF16),
            jax.ShapeDtypeStruct((rows, wide), F32),
        ),
        in_specs=[anywhere, anywhere, anywhere, vmem],
        out_specs=(anywhere, anywhere),
        scratch_shapes=[pltpu.VMEM((rows, wide), F32), pltpu.VMEM((slots, wide), F32), dma((2 + 2 * per_block,))],
        compiler_params=pltpu.CompilerParams(vmem_limit_bytes=limit),
        name="finish",
    )(part_act, part_grad, returned, row)


def solution(mesh):
    placed = (
        P(("dom", "src"), None),
        P(("dom", "src"), None),
        P(),
        P(),
        P(),
        P("dom", "src", None, None),
        P("dom", "src", None),
        P("dom", "src", None),
        P("dom", "src"),
    )
    return jax.shard_map(
        local,
        mesh=mesh,
        in_specs=placed,
        out_specs=(P(("dom", "src"), None), P(("dom", "src"), None)),
        check_vma=False,
    )
```

```python
import functools

import jax
import jax.numpy as jnp
from jax import lax
from jax.experimental import pallas as pl
from jax.experimental.pallas import tpu as pltpu
from jax.sharding import PartitionSpec as P

MESH = pl.DeviceIdType.MESH
CHUNK = 256
STRIP = 64
F32 = jnp.float32
BF16 = jnp.bfloat16


def strip_of(width):
    return max(rows for rows in range(16, 321, 16) if width % rows == 0)


def build_kernel(width, source_hbm, target_hbm, feature_hbm, sender_hbm, count_ref,
                 adjacency_ref, degree_ref, picked_ref, row_ref,
                 source_ref, target_ref, feature_ref, sender_ref, word_vmem, word_ref, keys, even, odd, stage,
                 in_sem, stage_sem, *tables):
    incoming = [
        pltpu.make_async_copy(source_hbm.at[0], source_ref, in_sem.at[0]),
        pltpu.make_async_copy(target_hbm.at[0], target_ref, in_sem.at[1]),
        pltpu.make_async_copy(feature_hbm, feature_ref, in_sem.at[2]),
        pltpu.make_async_copy(sender_hbm, sender_ref, in_sem.at[4]),
    ]
    for copy in incoming:
        copy.start()
    total_rows = tables[0].shape[0]
    lanes = len(tables)
    accounts = feature_ref.shape[0]
    per_block = accounts // CHUNK
    blocks = stage.shape[0] // per_block
    strip = strip_of(width)
    tiles = count_ref[0]

    incoming[0].wait()
    incoming[1].wait()
    edges = target_ref.shape[1]
    target = target_ref[...]
    within = target % accounts
    word_vmem[...] = (within // 128) * width + source_ref[...]
    word_copy = pltpu.make_async_copy(word_vmem, word_ref, in_sem.at[3])
    word_copy.start()
    key = (target // accounts) * 128 + within % 128
    for tile in range(edges // 128):
        keys[tile : tile + 1, :] = key[:, tile * 128 : tile * 128 + 128]

    zeros = jnp.zeros((128, 128), jnp.int32)

    def clear(chosen):
        def go(step, carry):
            for table in chosen:
                table[pl.ds(pl.multiple_of(step * 128, 128), 128), :] = zeros
            return carry

        lax.fori_loop(0, total_rows // 128, go, 0)

    clear(tables)
    word_copy.wait()
    incoming[2].wait()
    incoming[3].wait()

    lane_at = lax.broadcasted_iota(jnp.int32, (128, 128), 1)

    def one_hot(out, tile):
        held = jnp.minimum(tile, edges // 128 - 1)
        key = jnp.broadcast_to(keys[pl.ds(held, 1), :], (128, 128)).T
        amount = lax.shift_left(jnp.where(tile < tiles, 1, 0), lax.shift_right_logical(key, 7) * 8)
        out[...] = jnp.where(lane_at == (key & 127), amount, 0)

    def add_tile(rows_of, tile):
        base = jnp.minimum(tile, edges // 128 - 1) * 128
        for group in range(0, 128, lanes):
            rows = [pl.ds(word_ref[0, base + group + k], 1) for k in range(lanes)]
            sums = [tables[k][rows[k], :] + rows_of[group + k : group + k + 1, :] for k in range(lanes)]
            for k in range(lanes):
                tables[k][rows[k], :] = sums[k]

    def edge_tiles(pair, carry):
        one_hot(odd, 2 * pair + 1)
        add_tile(even, 2 * pair)
        one_hot(even, 2 * pair + 2)
        add_tile(odd, 2 * pair + 1)
        return carry

    one_hot(even, 0)
    lax.fori_loop(0, (tiles + 1) // 2, edge_tiles, 0)

    peers, capacity = sender_ref.shape[2:]
    slots = peers * capacity
    sender = sender_ref[0, 0]
    repeat = (
        lax.broadcasted_iota(jnp.int32, (capacity, slots), 1) % capacity
        == lax.broadcasted_iota(jnp.int32, (capacity, slots), 0)
    ).astype(F32).astype(BF16)
    high = jnp.dot(lax.shift_right_arithmetic(sender, 5).astype(F32).astype(BF16), repeat, preferred_element_type=F32)
    low = jnp.dot((sender & 31).astype(F32).astype(BF16), repeat, preferred_element_type=F32)
    mine = (
        lax.broadcasted_iota(jnp.int32, (peers, slots), 1) // capacity
        == lax.broadcasted_iota(jnp.int32, (peers, slots), 0)
    )
    row = jnp.sum(jnp.where(mine, high * 32.0 + low, 0.0), axis=0, keepdims=True).astype(jnp.int32)
    row_ref[...] = row
    chosen = lax.broadcasted_iota(jnp.int32, (accounts, slots), 0) == row
    picked_ref[...] = lax.dot_general(
        chosen.astype(F32).astype(BF16), feature_ref[...], (((0,), (0,)), ((), ())), preferred_element_type=F32
    )

    degree_ref[...] = jnp.zeros_like(degree_ref)

    def stage_copy(at):
        return pltpu.make_async_copy(stage.at[at], adjacency_ref.at[at], stage_sem.at[at])

    counted = jnp.zeros((8, 128), F32)
    for piece in range(per_block):
        for side in range(2):
            first = (2 * piece + side) * width
            columns = pl.ds(side * 128, 128)

            def unpack(step, sums, first=first, columns=columns, piece=piece):
                rows = pl.ds(pl.multiple_of(first + step * strip, 16), strip)
                packed = tables[0][rows, :]
                for table in tables[1:]:
                    packed = packed + table[rows, :]
                out = pl.ds(pl.multiple_of(step * strip, 16), strip)
                after = []
                for field in range(4):
                    value = packed if field == 0 else lax.shift_right_logical(packed, 8 * field)
                    value = (value if field == 3 else value & 255).astype(F32)
                    stage[field * per_block + piece, out, columns] = value.astype(BF16)
                    after.append(sums[field] + jnp.sum(value.reshape(strip // 8, 8, 128), axis=0))
                return tuple(after)

            sums = lax.fori_loop(0, width // strip, unpack, (jnp.zeros((8, 128), F32),) * 4)
            for field in range(4):
                degree_ref[field, pl.ds(piece, 1), columns] = jnp.sum(sums[field], axis=0, keepdims=True)
                counted = counted + sums[field]
        for field in range(4):
            stage_copy(field * per_block + piece).start()
    for at in range(blocks * per_block):
        stage_copy(at).wait()

    @pl.when(jnp.sum(counted).astype(jnp.int32) != tiles * 128)
    def _():
        table = tables[0]

        def field_pass(field, carry):
            clear(tables[:1])

            def one(edge, carry):
                rows = pl.ds(word_ref[0, edge], 1)
                amount = even[pl.ds(edge % 128, 1), :]
                match = lax.shift_right_logical(amount, 8 * field) & 255
                table[rows, :] = table[rows, :] + match
                return carry

            def tile_pass(tile, carry):
                one_hot(even, tile)
                return lax.fori_loop(tile * 128, tile * 128 + 128, one, carry)

            lax.fori_loop(0, tiles, tile_pass, 0)
            for piece in range(per_block):
                for side in range(2):
                    value = table[pl.ds((2 * piece + side) * width, width), :].astype(F32)
                    columns = pl.ds(side * 128, 128)
                    stage[field * per_block + piece, :, columns] = value.astype(BF16)
                    degree_ref[field, pl.ds(piece, 1), columns] = jnp.sum(value, axis=0, keepdims=True)
            return carry

        lax.fori_loop(0, 4, field_pass, 0)
        for at in range(blocks * per_block):
            stage_copy(at).start()
        for at in range(blocks * per_block):
            stage_copy(at).wait()


def layer_kernel(doms, adjacency_ref, degree_ref, picked_ref, feature_hbm, cotangent_hbm, self_hbm, neigh_hbm,
                 bias_hbm, act_hbm, grad_hbm, returned_hbm,
                 feature_ref, cotangent_ref, self_ref, neigh_ref, bias_ref, act_ref, grad_ref,
                 adjacency, table_t, halo, halo_t, degree_in, inverse, own_pre,
                 foreign, kept, to_sibling, from_sibling, chip_out, chip_in, own_out, own_in, spread,
                 halo_grad, returned,
                 in_sem, out_sem, load_sem, halo_send, halo_recv, degree_send, degree_recv, part_send, part_recv, grad_send, grad_recv,
                 back_send, back_recv):
    part, source = lax.axis_index("dom"), lax.axis_index("src")
    chip, core = source // 2, source % 2
    sibling = chip * 2 + (1 - core)
    opposite = (1 - chip) * 2 + core
    diagonal = (1 - chip) * 2 + (1 - core)
    rows = feature_ref.shape[0]
    per_block = rows // CHUNK
    capacity = halo.shape[0] // doms

    barrier = pltpu.get_barrier_semaphore()
    for step in range(1, 4):
        pl.semaphore_signal(barrier, inc=1, device_id=(part, lax.rem(source + step, 4)), device_id_type=MESH)

    def greet(step, carry):
        pl.semaphore_signal(barrier, inc=1, device_id=(lax.rem(part + step, doms), source), device_id_type=MESH)
        return carry

    lax.fori_loop(1, doms, greet, 0)

    def load(chunk):
        return pltpu.make_async_copy(adjacency_ref.at[chunk], adjacency.at[chunk], load_sem.at[chunk])

    def load_block(block):
        def go(step, carry):
            load(block * per_block + step).start()
            return carry

        lax.fori_loop(0, per_block, go, 0)

    incoming = [
        pltpu.make_async_copy(whole, here, in_sem.at[at])
        for at, (whole, here) in enumerate((
            (feature_hbm, feature_ref), (self_hbm, self_ref), (neigh_hbm, neigh_ref), (bias_hbm, bias_ref),
            (cotangent_hbm, cotangent_ref), (degree_ref.at[source], degree_in.at[0]),
        ))
    ]
    incoming[0].start()
    load_block(diagonal)
    load_block(opposite)
    pl.semaphore_wait(barrier, 3 + doms - 1)

    def slot(at):
        return pl.ds(pl.multiple_of(at * capacity, capacity), capacity)

    def halo_copy(step):
        peer = lax.rem(part + step, doms)
        return pltpu.make_async_remote_copy(
            src_ref=picked_ref.at[slot(peer)], dst_ref=halo.at[slot(part)],
            send_sem=halo_send.at[step], recv_sem=halo_recv.at[step],
            device_id=(peer, source), device_id_type=MESH)

    def back_copy(step):
        peer = lax.rem(part + step, doms)
        return pltpu.make_async_remote_copy(
            src_ref=halo_grad.at[slot(peer)], dst_ref=returned.at[slot(part)],
            send_sem=back_send.at[step], recv_sem=back_recv.at[step],
            device_id=(peer, source), device_id_type=MESH)

    def each_peer(action):
        def go(step, carry):
            action(step)
            return carry

        lax.fori_loop(1, doms, go, 0)

    each_peer(lambda step: halo_copy(step).start())

    def degree_copy(step):
        peer = lax.rem(source + step, 4)
        return pltpu.make_async_remote_copy(
            src_ref=degree_ref.at[peer], dst_ref=degree_in.at[step],
            send_sem=degree_send.at[step], recv_sem=degree_recv.at[step],
            device_id=(part, peer), device_id_type=MESH)

    for step in range(1, 4):
        degree_copy(step).start()
    for copy in incoming[1:]:
        copy.start()
    load_block(sibling)
    load_block(source)
    incoming[0].wait()
    table_t[...] = feature_ref[...].astype(F32).T.astype(BF16)

    def part_copy(kind, step):
        source_ref, target_ref, peer = (
            (to_sibling, from_sibling, sibling),
            (chip_out, chip_in, opposite),
            (own_out, own_in, sibling),
        )[kind]
        return pltpu.make_async_remote_copy(
            src_ref=source_ref.at[step], dst_ref=target_ref.at[step],
            send_sem=part_send.at[kind, step], recv_sem=part_recv.at[kind, step],
            device_id=(part, peer), device_id_type=MESH)

    def grad_copy(kind, step):
        owner, peer = ((source, sibling), (source, opposite), (opposite, sibling))[kind]
        at = owner * per_block + step
        return pltpu.make_async_remote_copy(
            src_ref=spread.at[at], dst_ref=spread.at[at],
            send_sem=grad_send.at[kind, step], recv_sem=grad_recv.at[kind, step],
            device_id=(part, peer), device_id_type=MESH)

    def each_chunk(action):
        def go(step, carry):
            action(step)
            return carry

        lax.fori_loop(0, per_block, go, 0)

    def from_local(at):
        return jnp.dot(table_t[...], adjacency[at, 0:rows, :], preferred_element_type=F32)

    def from_halo(at):
        return jnp.dot(halo_t[...], adjacency[at, rows:, :], preferred_element_type=F32)

    def early(step):
        at = diagonal * per_block + step
        load(at).wait()
        foreign[step] = from_local(at)

    def early_kept(step):
        at = opposite * per_block + step
        load(at).wait()
        kept[step] = from_local(at)

    for step in range(2):
        early(step)
        early_kept(step)
    halo[slot(part), :] = jnp.zeros((capacity, halo.shape[1]), F32)
    returned[slot(part), :] = jnp.zeros((capacity, halo.shape[1]), F32)
    each_peer(lambda step: halo_copy(step).wait_recv())
    halo_t[...] = halo[...].T.astype(BF16)

    def send_foreign(step):
        to_sibling[step] = (foreign[step] + from_halo(diagonal * per_block + step)).astype(BF16)
        part_copy(0, step).start()

    send_foreign(0)
    send_foreign(1)
    for step in range(2, per_block):
        early(step)
        send_foreign(step)

    def send_chip(step):
        mine = kept[step] + from_halo(opposite * per_block + step)
        part_copy(0, step).wait_recv()
        chip_out[step] = (mine + from_sibling[step].astype(F32)).astype(BF16)
        part_copy(1, step).start()

    send_chip(0)
    send_chip(1)
    for step in range(2, per_block):
        early_kept(step)

    def send_own(step):
        at = sibling * per_block + step
        load(at).wait()
        own_out[step] = (from_local(at) + from_halo(at)).astype(BF16)
        part_copy(2, step).start()

    each_chunk(send_own)

    def keep_own(step):
        at = source * per_block + step
        load(at).wait()
        foreign[step] = from_local(at) + from_halo(at)

    each_chunk(keep_own)
    for copy in incoming[1:]:
        copy.wait()
    own_pre[...] = jnp.dot(feature_ref[...], self_ref[...], preferred_element_type=F32) + bias_ref[...].astype(F32).reshape(1, -1)

    degree = degree_in[0]
    for step in range(1, 4):
        degree_copy(step).wait_recv()
        degree = degree + degree_in[step]
    inverse[...] = 1.0 / jnp.maximum(degree, 1.0)
    halo_grad[...] = jnp.zeros_like(halo_grad)
    grad_ref[...] = jnp.zeros_like(grad_ref)

    def back_halo(at):
        halo_grad[...] += jnp.dot(adjacency[at, rows:, :], spread[at], preferred_element_type=F32)

    def back_local(at):
        grad_ref[...] += jnp.dot(adjacency[at, 0:rows, :], spread[at], preferred_element_type=F32)

    def back_own(step):
        at = source * per_block + step
        back_halo(at)
        back_local(at)

    def back_sibling(step):
        at = sibling * per_block + step
        grad_copy(0, step).wait_recv()
        back_halo(at)
        back_local(at)

    def act_copy(step):
        here = pl.ds(pl.multiple_of(step * CHUNK, CHUNK), CHUNK)
        return pltpu.make_async_copy(act_ref.at[here], act_hbm.at[here], out_sem.at[step])

    def dense(step):
        here = pl.ds(pl.multiple_of(step * CHUNK, CHUNK), CHUNK)
        inverse_row = inverse[pl.ds(step, 1), :]
        half = jnp.broadcast_to(inverse_row, (128, CHUNK)).T
        inverse_column = jnp.concatenate([half] * (act_ref.shape[1] // 128), axis=1)
        part_copy(2, step).wait_recv()
        part_copy(1, step).wait_recv()
        total_t = foreign[step] + own_in[step].astype(F32) + chip_in[step].astype(F32)
        mean = (total_t * inverse_row).T.astype(BF16)
        preact = own_pre[here, :] + jnp.dot(mean, neigh_ref[...], preferred_element_type=F32)
        sigma = jax.nn.sigmoid(preact)
        slope = sigma * (1.0 + preact * (1.0 - sigma))
        upstream = (cotangent_ref[here, :].astype(F32) * slope).astype(BF16)
        contract = (((1,), (1,)), ((), ()))
        at = source * per_block + step
        spread[at] = (
            lax.dot_general(upstream, neigh_ref[...], contract, preferred_element_type=F32) * inverse_column
        ).astype(BF16)
        grad_copy(1, step).start()
        grad_copy(0, step).start()
        act_ref[here, :] = (preact * sigma).astype(BF16)
        act_copy(step).start()
        grad_ref[here, :] += lax.dot_general(upstream, self_ref[...], contract, preferred_element_type=F32)

    for step in range(2, per_block):
        part_copy(1, step - 2).wait_send()
        send_chip(step)
        dense(step - 2)
        back_own(step - 2)
    for step in range(per_block - 2, per_block):
        grad_copy(1, step - 2).wait_send()
        dense(step)
        back_own(step)
    for step in range(per_block):
        back_sibling(step)
    last = per_block - 1
    for step in range(per_block):
        grad_copy(1, step).wait_recv()
        grad_copy(2, step).start()
        back_halo(opposite * per_block + step)
        if step < last:
            back_local(opposite * per_block + step)
        if step > 0:
            grad_copy(2, step - 1).wait_recv()
            back_halo(diagonal * per_block + step - 1)
            back_local(diagonal * per_block + step - 1)
    grad_copy(2, last).wait_recv()
    back_halo(diagonal * per_block + last)
    each_peer(lambda step: back_copy(step).start())
    back_local(opposite * per_block + last)
    back_local(diagonal * per_block + last)

    grad_out = pltpu.make_async_copy(grad_ref, grad_hbm, out_sem.at[per_block])
    grad_out.start()
    each_peer(lambda step: back_copy(step).wait_recv())
    returned_out = pltpu.make_async_copy(returned, returned_hbm, out_sem.at[per_block + 1])
    returned_out.start()
    each_peer(lambda step: halo_copy(step).wait_send())
    each_peer(lambda step: back_copy(step).wait_send())
    for step in range(1, 4):
        degree_copy(step).wait_send()
    each_chunk(lambda step: act_copy(step).wait())
    for kind in range(3):
        for step in range(per_block - 2 if kind == 1 else 0, per_block):
            part_copy(kind, step).wait_send()
            grad_copy(kind, step).wait_send()
    grad_out.wait()
    returned_out.wait()


def finish_kernel(part_act_ref, part_grad_ref, returned_ref, row_ref, act_ref, grad_ref, act, grad, returned, sem):
    pieces = grad_ref.shape[0] // CHUNK

    def piece(at):
        return pl.ds(at * CHUNK, CHUNK)

    act_in = pltpu.make_async_copy(part_act_ref, act, sem.at[0])
    act_out = pltpu.make_async_copy(act, act_ref, sem.at[0])
    back = pltpu.make_async_copy(returned_ref, returned, sem.at[1])
    come = [
        pltpu.make_async_copy(part_grad_ref.at[piece(at)], grad.at[piece(at)], sem.at[2 + at]) for at in range(pieces)
    ]
    back.start()
    for copy in come:
        copy.start()
    act_in.start()
    back.wait()
    rows = returned[...].astype(BF16)
    leave = []
    for at in range(pieces):
        chosen = lax.broadcasted_iota(jnp.int32, (CHUNK, row_ref.shape[1]), 0) + at * CHUNK == row_ref[...]
        added = jnp.dot(chosen.astype(F32).astype(BF16), rows, preferred_element_type=F32)
        come[at].wait()
        grad[piece(at), :] += added
        leave.append(pltpu.make_async_copy(grad.at[piece(at)], grad_ref.at[piece(at)], sem.at[2 + pieces + at]))
        leave[-1].start()
    act_in.wait()
    act_out.start()
    act_out.wait()
    for copy in leave:
        copy.wait()


def local(features, cotangent, w_self, w_neigh, bias, send_rows, edge_src, edge_dst, tile_count):
    rows, features_wide = features.shape
    doms, columns = lax.axis_size("dom"), lax.axis_size("src")
    slots = send_rows.shape[2] * send_rows.shape[3]
    width = rows + slots
    chunks = rows * columns // CHUNK
    per_block = rows // CHUNK
    edges = edge_src.shape[2]
    limit = 58 * 1024 * 1024
    vmem = pl.BlockSpec(memory_space=pltpu.VMEM)
    smem = pl.BlockSpec(memory_space=pltpu.SMEM)
    anywhere = pl.BlockSpec(memory_space=pl.ANY)
    hbm = pl.BlockSpec(memory_space=pltpu.HBM)

    adjacency, degree, picked, row = pl.pallas_call(
        functools.partial(build_kernel, width),
        out_shape=(
            jax.ShapeDtypeStruct((chunks, width, CHUNK), BF16),
            jax.ShapeDtypeStruct((columns, 8, CHUNK), F32),
            jax.ShapeDtypeStruct((slots, features_wide), F32),
            jax.ShapeDtypeStruct((1, slots), jnp.int32),
        ),
        in_specs=[hbm, hbm, hbm, hbm, smem],
        out_specs=(anywhere, vmem, vmem, vmem),
        scratch_shapes=[
            pltpu.VMEM((1, edges), jnp.int32),
            pltpu.VMEM((1, edges), jnp.int32),
            pltpu.VMEM((rows, features_wide), BF16),
            pltpu.VMEM(send_rows.shape, jnp.int32),
            pltpu.VMEM((1, edges), jnp.int32),
            pltpu.SMEM((1, edges), jnp.int32),
            pltpu.VMEM((edges // 128, 128), jnp.int32),
            pltpu.VMEM((128, 128), jnp.int32),
            pltpu.VMEM((128, 128), jnp.int32),
            pltpu.VMEM((chunks, width, CHUNK), BF16),
            pltpu.SemaphoreType.DMA((5,)),
            pltpu.SemaphoreType.DMA((chunks,)),
        ] + [pltpu.VMEM((rows // 128 * width, 128), jnp.int32)] * 4,
        compiler_params=pltpu.CompilerParams(vmem_limit_bytes=limit),
        name="count_edges",
    )(edge_src, edge_dst, features, send_rows, tile_count.reshape(1))

    wide = features_wide
    dma = pltpu.SemaphoreType.DMA
    block_half = pltpu.VMEM((per_block, wide, CHUNK), BF16)
    block_full = pltpu.VMEM((per_block, wide, CHUNK), F32)
    part_act, part_grad, returned = pl.pallas_call(
        functools.partial(layer_kernel, doms),
        out_shape=(
            jax.ShapeDtypeStruct((rows, wide), BF16),
            jax.ShapeDtypeStruct((rows, wide), F32),
            jax.ShapeDtypeStruct((slots, wide), F32),
        ),
        in_specs=[anywhere] * 3 + [hbm] * 5,
        out_specs=(anywhere, anywhere, anywhere),
        scratch_shapes=[
            pltpu.VMEM((rows, wide), BF16),
            pltpu.VMEM((rows, wide), BF16),
            pltpu.VMEM(w_self.shape, BF16),
            pltpu.VMEM(w_neigh.shape, BF16),
            pltpu.VMEM(bias.shape, BF16),
            pltpu.VMEM((rows, wide), BF16),
            pltpu.VMEM((rows, wide), F32),
            pltpu.VMEM((chunks, width, CHUNK), BF16),
            pltpu.VMEM((wide, rows), BF16),
            pltpu.VMEM((slots, wide), F32),
            pltpu.VMEM((wide, slots), BF16),
            pltpu.VMEM((4, 8, CHUNK), F32),
            pltpu.VMEM((8, CHUNK), F32),
            pltpu.VMEM((rows, wide), F32),
            block_full, block_full,
            block_half, block_half, block_half, block_half, block_half, block_half,
            pltpu.VMEM((chunks, CHUNK, wide), BF16),
            pltpu.VMEM((slots, wide), F32),
            pltpu.VMEM((slots, wide), F32),
            dma((6,)), dma((per_block + 2,)), dma((chunks,)),
            dma((doms,)), dma((doms,)),
            dma((4,)), dma((4,)),
            dma((3, per_block)), dma((3, per_block)),
            dma((3, per_block)), dma((3, per_block)),
            dma((doms,)), dma((doms,)),
        ],
        compiler_params=pltpu.CompilerParams(
            collective_id=0, has_side_effects=True, vmem_limit_bytes=limit
        ),
        name="layer",
    )(adjacency, degree, picked, features, cotangent, w_self, w_neigh, bias)

    return pl.pallas_call(
        finish_kernel,
        out_shape=(
            jax.ShapeDtypeStruct((rows, wide), BF16),
            jax.ShapeDtypeStruct((rows, wide), F32),
        ),
        in_specs=[anywhere, anywhere, anywhere, vmem],
        out_specs=(anywhere, anywhere),
        scratch_shapes=[
            pltpu.VMEM((rows, wide), BF16),
            pltpu.VMEM((rows, wide), F32),
            pltpu.VMEM((slots, wide), F32),
            dma((2 + 2 * per_block,)),
        ],
        compiler_params=pltpu.CompilerParams(vmem_limit_bytes=limit),
        name="finish",
    )(part_act, part_grad, returned, row)


def solution(mesh):
    placed = (
        P(("dom", "src"), None),
        P(("dom", "src"), None),
        P(),
        P(),
        P(),
        P("dom", "src", None, None),
        P("dom", "src", None),
        P("dom", "src", None),
        P("dom", "src"),
    )
    return jax.shard_map(
        local,
        mesh=mesh,
        in_specs=placed,
        out_specs=(P(("dom", "src"), None), P(("dom", "src"), None)),
        check_vma=False,
    )
```
